32 devices in a mesh: section: 2 (over x), fsdp: 4 (over z), seq: 4 (over y, core).
Axes of the slice: x: 2, y: 2, z: 4, core: 2. Of those that a mesh axis runs over, the one named last changes fastest.
Arguments:
- acts: bfloat16 [2, 4, 512, 1536], P('section', 'fsdp', 'seq')
- grad_out: bfloat16 [4, 512, 1536], P('fsdp', 'seq'), may hold values from -6 to 6
- gain: float32 [2, 1536], P('section'), may hold values from 0.5 to 2
- gate: float32 [2, 1536], P('section'), may hold values from 0.5 to 2
- w_query: bfloat16 [2, 1536, 1536], P('section', ('fsdp', 'seq'))
- kept: int32 [4, 2], P('fsdp'), may hold values from 0 to 1, as said below
- links: int32 [4, 4], P('fsdp', 'seq'), may hold values from 0 to 1, as said below
Outputs:
- grad_acts: bfloat16 [2, 4, 512, 1536], P('section', 'fsdp', 'seq')
- grad_wq: bfloat16 [2, 1536, 1536], P('section', ('fsdp', 'seq'))
The draws below stay inside these ranges and needn't reach their ends.
Inputs may be any that keep to these rules, and one draw needn't show every extreme that they name: `kept`: clip 0 runs every layer; the other entries vary. `links`: in clip 0 every tile after the first attends the tile before it; the other entries vary.
All inputs are finite; a program needn't handle non-finite values.
Results may differ from the reference program's by a relative error of at most 0.025.
The reference program's roundings to bfloat16 on the way count: a program that leaves them out, or rounds other values in their place, can miss the bound.
Values may be sent and summed in bfloat16 or wider, within the bound.
No kernel may reach another device: no remote copies, remote signals or barrier semaphores. Data moves between devices by JAX's collectives and lax.ppermute only.
A program may use at most 64 MiB of HBM per device.

```python
import math
import jax
import jax.numpy as jnp
from jax import lax

D = 1536
HDIM = 128
TILE = 128
HEADS = 12
LAYERS = 2
CLIPS = 4
TILES = 4
TOKC = 512


def draw_acts(key, part):
    key_main = jax.random.fold_in(key, 0)
    full_shape = (LAYERS, CLIPS, TOKC, D)
    values_drawn = jax.random.normal(key_main, full_shape, jnp.float32)
    return values_drawn.astype(jnp.bfloat16)


def draw_w_query(key, part):
    key_main = jax.random.fold_in(key, 0)
    matrix = jax.random.normal(key_main, (LAYERS, D, D), jnp.float32) * D ** (-0.5)
    return matrix.astype(jnp.bfloat16)


def draw_kept(key, part):
    drawn = (jax.random.randint(jax.random.fold_in(key, 11), (CLIPS, LAYERS), 0, 4) > 0).astype(jnp.int32)
    first_clip = (lax.broadcasted_iota(jnp.int32, (CLIPS, LAYERS), 0) == 0).astype(jnp.int32)
    return jnp.maximum(drawn, first_clip)


def draw_links(key, part):
    drawn = jax.random.randint(jax.random.fold_in(key, 23), (CLIPS, TILES), 0, 2)
    first_clip = (lax.broadcasted_iota(jnp.int32, (CLIPS, TILES), 0) == 0).astype(jnp.int32)
    return jnp.maximum(drawn, first_clip).astype(jnp.int32)


def shard_levels(stream_key, dims, cuts, low, largest):
    def one(position, shards_of):
        heights = jax.random.uniform(jax.random.fold_in(jax.random.fold_in(stream_key, 6), position), (shards_of,), jnp.float32, low / len(cuts), largest / len(cuts))
        return jnp.repeat(jnp.exp(heights), dims[position] // shards_of).reshape((-1,) + (1,) * (len(dims) - position - 1))

    factor_of = one(*cuts[0])
    for cut in cuts[1:]:
        factor_of = factor_of * one(*cut)
    return factor_of


def normal_values(stream_key, dims, deviation, reach, shards=(), held_as=jnp.bfloat16):
    result = jax.random.normal(stream_key, dims, jnp.float32) * deviation
    if len(shards) > 0:
        result = shard_levels(stream_key, dims, shards, -0.22, 0.18) * result
    return jnp.clip(result, min=-reach, max=reach).astype(held_as)


def setup_inputs(seed: int = 0) -> dict:
    arg_keys = jax.random.split(jax.random.key(seed), 8)
    return {
        "acts": draw_acts(jax.random.fold_in(arg_keys[7], 71), 0),
        "grad_out": normal_values(arg_keys[1], (CLIPS, TOKC, D), 1.0, 6.0, ((0, 4), (1, 4))),
        "gain": jnp.clip(jnp.exp(math.log(2.0) - 1.3862944 * jax.random.uniform(arg_keys[2], (LAYERS, D), jnp.float32) ** shard_levels(arg_keys[2], (LAYERS, D), ((0, 2),), -0.2, 0.2)), 0.5, 2.0),
        "gate": jnp.clip(jnp.exp(math.log(2.0) - 1.3862944 * jax.random.uniform(arg_keys[3], (LAYERS, D), jnp.float32) ** shard_levels(arg_keys[3], (LAYERS, D), ((0, 2),), -0.2, 0.2)), 0.5, 2.0),
        "w_query": draw_w_query(jax.random.fold_in(arg_keys[7], 71), 0),
        "kept": draw_kept(jax.random.fold_in(arg_keys[7], 71), 0),
        "links": draw_links(jax.random.fold_in(arg_keys[7], 71), 0),
    }


norm_eps = 1e-06

def clip_backward(x_clip, dy_clip, keep_flag, links, gain_row, gate_row, weights):
    tile_count = TILES
    x_rows = x_clip.astype(jnp.float32).reshape(tile_count, TILE, D)
    inv_rms = lax.rsqrt(lax.optimization_barrier(jnp.mean(x_rows * x_rows, axis=-1, keepdims=True)) + norm_eps)
    normed = (x_rows * inv_rms * gain_row).astype(jnp.bfloat16)
    query_rows = jnp.dot(normed.reshape(tile_count * TILE, D), weights, preferred_element_type=jnp.float32)
    query_rows = query_rows.astype(jnp.bfloat16).reshape(tile_count, TILE, D)
    left_normed = jnp.concatenate([jnp.zeros_like(normed[:1]), normed[:-1]], axis=0)
    key_rows = jnp.concatenate([left_normed, normed], axis=1)
    positions = jnp.arange(tile_count, dtype=jnp.int32)
    linked = links * (positions > 0).astype(jnp.int32) > 0
    key_valid = jnp.concatenate([jnp.broadcast_to(linked[:, None], (tile_count, TILE)), jnp.ones((tile_count, TILE), dtype=jnp.bool_)], axis=1)
    score_scale = HDIM ** (-0.5)
    query_heads = query_rows.reshape(tile_count, TILE, HEADS, HDIM).astype(jnp.float32)
    key_heads = key_rows.reshape(tile_count, 2 * TILE, HEADS, HDIM).astype(jnp.float32)
    dy_tiles = dy_clip.reshape(tile_count, TILE, D)
    dy_float = dy_tiles.astype(jnp.float32)
    out_grad = (gate_row * dy_float).astype(jnp.bfloat16)
    grad_heads = out_grad.reshape(tile_count, TILE, HEADS, HDIM).astype(jnp.float32)
    scores = jnp.einsum('tihd,tjhd->thij', query_heads, key_heads) * score_scale
    scores = jnp.where(key_valid[:, None, None, :], scores, -1e+30)
    row_max = lax.optimization_barrier(jnp.max(scores, axis=-1, keepdims=True))
    exp_scores = jnp.exp(scores - row_max)
    prob_rows = exp_scores / lax.optimization_barrier(jnp.sum(exp_scores, axis=-1, keepdims=True))
    probs_low = lax.optimization_barrier(prob_rows.astype(jnp.bfloat16)).astype(jnp.float32)
    prob_grad = jnp.einsum('tihd,tjhd->thij', grad_heads, key_heads)
    row_delta = lax.optimization_barrier(jnp.sum(prob_rows * prob_grad, axis=-1, keepdims=True))
    score_grad = lax.optimization_barrier((prob_rows * (prob_grad - row_delta) * score_scale).astype(jnp.bfloat16)).astype(jnp.float32)
    query_grad = jnp.einsum('thij,tjhd->tihd', score_grad, key_heads).astype(jnp.bfloat16).reshape(tile_count, TILE, D)
    key_grad = jnp.einsum('thij,tihd->tjhd', score_grad, query_heads) + jnp.einsum('thij,tihd->tjhd', probs_low, grad_heads)
    key_grad = key_grad.reshape(tile_count, 2 * TILE, D)
    left_return = lax.optimization_barrier(key_grad[:, :TILE].astype(jnp.bfloat16)).astype(jnp.float32)
    from_right = jnp.concatenate([left_return[1:], jnp.zeros_like(left_return[:1])], axis=0)
    normed_grad = jnp.dot(query_grad.reshape(tile_count * TILE, D), weights.T, preferred_element_type=jnp.float32).reshape(tile_count, TILE, D)
    normed_grad = normed_grad + key_grad[:, TILE:] + from_right
    scaled_grad = normed_grad * gain_row
    mean_term = lax.optimization_barrier(jnp.mean(x_rows * scaled_grad, axis=-1, keepdims=True))
    change = inv_rms * (scaled_grad - x_rows * inv_rms * inv_rms * mean_term)
    updated = jnp.where(keep_flag > 0, (dy_float + change).astype(jnp.bfloat16), dy_tiles)
    tile_terms = jnp.einsum('tia,tib->tab', normed.astype(jnp.float32), query_grad.astype(jnp.float32))
    tile_terms = lax.optimization_barrier(tile_terms.astype(jnp.bfloat16)).astype(jnp.float32)
    weight_term = jnp.where(keep_flag > 0, lax.optimization_barrier(jnp.sum(tile_terms, axis=0)), jnp.zeros((D, D), jnp.float32))
    return (updated.reshape(tile_count * TILE, D), weight_term)

def reference(acts, grad_out, gain, gate, w_query, kept, links):
    dy_all = grad_out
    grad_list = [None] * LAYERS
    weight_list = [None] * LAYERS
    for section_index in reversed(range(LAYERS)):

        def one_clip(operands, section_index=section_index):
            x_clip, dy_clip, keep_flag, link_row = operands
            return clip_backward(x_clip, dy_clip, keep_flag, link_row, gain[section_index], gate[section_index], w_query[section_index])
        updated, weight_terms = lax.map(one_clip, (acts[section_index], dy_all, kept[:, section_index], links))
        grad_list[section_index] = updated
        weight_list[section_index] = lax.optimization_barrier(jnp.sum(weight_terms, axis=0)).astype(jnp.bfloat16)
        dy_all = updated
    return (jnp.stack(grad_list, axis=0), jnp.stack(weight_list, axis=0))
```

```python
import jax
import jax.numpy as jnp
from jax import lax
from jax.experimental import pallas as pl
from jax.experimental.pallas import tpu as pltpu
from jax.sharding import PartitionSpec as P

HDIM = 128
SCALE = HDIM ** (-0.5)
EPS = 1e-06
NEG = -1e30
BF = jnp.bfloat16
F32 = jnp.float32
VLIMIT = 16 * 1024 * 1024

NN = (((1,), (0,)), ((), ()))
NT = (((1,), (1,)), ((), ()))
TN = (((0,), (0,)), ((), ()))


def mm(a, b, dims):
    return lax.dot_general(a, b, dims, preferred_element_type=F32)


def sds(shape, dtype):
    return jax.ShapeDtypeStruct(shape, dtype)


def call(kernel, outs, flops, name, kept, links, *args, scratch=()):
    nbytes = sum(s.size * s.dtype.itemsize for s in outs) + sum(a.size * a.dtype.itemsize for a in args)
    return pl.pallas_call(
        kernel,
        out_shape=outs,
        in_specs=[pl.BlockSpec(memory_space=pltpu.SMEM)] * 2
        + [pl.BlockSpec(memory_space=pltpu.VMEM)] * len(args),
        out_specs=[pl.BlockSpec(memory_space=pltpu.VMEM)] * len(outs),
        scratch_shapes=list(scratch),
        compiler_params=pltpu.CompilerParams(vmem_limit_bytes=VLIMIT),
        cost_estimate=pl.CostEstimate(flops=flops, bytes_accessed=nbytes, transcendentals=0),
        name=name,
    )(kept, links, *args)


def where_am_i(kept, links):
    section = lax.axis_index("section")
    side = lax.rem(section, 2)
    hi = section - side + 1
    linked = jnp.logical_and(links[0, 0] > 0, lax.axis_index("seq") > 0)
    return side, linked, kept[0, hi] > 0, kept[0, hi - 1] > 0


def pick(side, value, half, other=False):
    first = value[:, :half]
    second = value[:, half:]
    use_first = (side == 1) if other else (side == 0)
    return jnp.where(use_first, first, second)


def hi_of(side, own, other):
    return jnp.where(side == 1, own[...], other[...])


def lo_of(side, own, other):
    return jnp.where(side == 1, other[...], own[...])


def inverse_rms(x):
    return lax.rsqrt(jnp.mean(x * x, axis=-1, keepdims=True) + EPS)


def select_kernel(kept, links, own, other, hi, lo):
    side, _, _, _ = where_am_i(kept, links)
    hi[...] = hi_of(side, own, other)
    lo[...] = lo_of(side, own, other)


def normalize_kernel(offsets, rows, kept, links, acts, acts_in, vecs, vecs_in, dy_full, *outs):
    normed, keys, parts = outs[:2], outs[2], outs[3 : 3 + len(offsets)]
    dy, turned = outs[-2], outs[-1]
    tile, half = dy.shape
    seqs = len(offsets)
    block = parts[0].shape[0] // 2
    side, _, _, _ = where_am_i(kept, links)
    seq = lax.axis_index("seq")
    for which, select in enumerate((hi_of, lo_of)):
        x = select(side, acts, acts_in).astype(F32)
        gain = select(side, vecs, vecs_in)[:1]
        value = (x * inverse_rms(x) * gain).astype(BF)
        normed[which][...] = value
        keys[which * tile : (which + 1) * tile, :] = pick(side, value, half)
        turned[...] = value.astype(F32).T.astype(BF)
        for part, offset in zip(parts, offsets):
            for f in range(block // rows):
                source = pl.multiple_of((f * seqs + jnp.bitwise_xor(seq, offset)) * rows, rows)
                target = which * block + f * rows
                part[target : target + rows, :] = turned[pl.ds(source, rows), :]
    dy[...] = pick(side, dy_full[...], half)


def head_probs(query, keys, linked):
    scores = mm(query, keys, NT) * SCALE
    column = lax.broadcasted_iota(jnp.int32, scores.shape, 1)
    scores = jnp.where(jnp.logical_or(column >= scores.shape[1] // 2, linked), scores, NEG)
    exps = jnp.exp(scores - jnp.max(scores, axis=-1, keepdims=True))
    return exps / jnp.sum(exps, axis=-1, keepdims=True)


def head_backward(query, keys, grads, probs):
    prob_grad = mm(grads, keys, NT)
    row_delta = jnp.sum(probs * prob_grad, axis=-1, keepdims=True)
    score_grad = (probs * (prob_grad - row_delta) * SCALE).astype(BF)
    query_grad = mm(score_grad, keys, NN).astype(BF)
    key_grad = mm(
        jnp.concatenate([score_grad, probs.astype(BF)], axis=0),
        jnp.concatenate([query, grads], axis=0),
        TN,
    )
    return query_grad, key_grad


def pieces(column):
    high = column.astype(BF)
    rest = column - high.astype(F32)
    middle = rest.astype(BF)
    low = (rest - middle.astype(F32)).astype(BF)
    rows = column.shape[0]
    lane = lax.broadcasted_iota(jnp.int32, (rows, HDIM), 1)
    high, middle, low = [jnp.broadcast_to(p.astype(F32), (rows, HDIM)) for p in (high, middle, low)]
    value = jnp.where(lane == 0, high, jnp.where(lane == 1, middle, jnp.where(lane == 2, low, 0.0)))
    return value.astype(BF)


def unpieces(block):
    return jnp.sum(block.astype(F32), axis=-1, keepdims=True)


def heads_of(half):
    return [slice(h * HDIM, (h + 1) * HDIM) for h in range(half // HDIM)]


def pairs_of(half):
    step = 2 * HDIM if half % (2 * HDIM) == 0 else HDIM
    return [slice(c, c + step) for c in range(0, half, step)]


def forward_kernel(which, places, rows, kept, links, normed, left_keys, own_keys, *rest):
    blocks = rest[: len(places)]
    query_out, probs_out, weights = rest[len(places) :]
    tile, half = query_out.shape
    token = slice(which * tile, (which + 1) * tile)
    _, linked, _, _ = where_am_i(kept, links)
    fsdps = lax.axis_size("fsdp")
    seqs = lax.axis_size("seq")
    fsdp, seq = lax.axis_index("fsdp"), lax.axis_index("seq")
    for block, place in zip(blocks, places):
        for index, (shift, offset) in enumerate(place):
            f = lax.rem(fsdp - shift + fsdps, fsdps)
            target = pl.multiple_of((f * seqs + jnp.bitwise_xor(seq, offset)) * rows, rows)
            weights[pl.ds(target, rows), :] = block[index * rows : (index + 1) * rows, :]
    tokens = normed[...]
    for cols in pairs_of(half):
        query = mm(tokens, weights[:, cols], NN).astype(BF)
        query_out[:, cols] = query
        for sub in heads_of(cols.stop - cols.start):
            at = slice(cols.start + sub.start, cols.start + sub.stop)
            keys = jnp.concatenate([left_keys[token, at], own_keys[token, at]], axis=0)
            start = at.start // HDIM * tile
            probs_out[start : start + tile, :] = head_probs(query[:, sub], keys, linked)


def upper_kernel(
    kept, links, dy, acts, acts_in, vecs, vecs_in, query, probs, weights, left_keys, own_keys,
    qg, own, msg, leftward, leftsum,
):
    tile, half = dy.shape
    side, _, keep, _ = where_am_i(kept, links)
    gate = pick(side, hi_of(side, vecs, vecs_in)[1:2], half)
    gain = hi_of(side, vecs, vecs_in)[:1]
    grads = (gate * dy[...].astype(F32)).astype(BF)
    left_total = jnp.zeros((tile, 1), F32)
    for at in heads_of(half):
        left = left_keys[:tile, at]
        keys = jnp.concatenate([left, own_keys[:tile, at]], axis=0)
        start = at.start // HDIM * tile
        query_grad, key_grad = head_backward(query[:, at], keys, grads[:, at], probs[start : start + tile, :])
        qg[:, at] = jnp.where(keep, query_grad, jnp.zeros_like(query_grad))
        back = key_grad[:tile].astype(BF)
        leftward[:, at] = back
        left_total += jnp.sum(back.astype(F32) * left.astype(F32), axis=-1, keepdims=True)
        own[:, at] = key_grad[tile:]
    leftsum[...] = jnp.broadcast_to(left_total, leftsum.shape)
    part = mm(qg[...], weights[...], NT)
    x_gain = hi_of(side, acts, acts_in).astype(F32) * gain
    total = jnp.sum(x_gain * part, axis=-1, keepdims=True)
    total += jnp.sum(pick(side, x_gain, half) * own[...], axis=-1, keepdims=True)
    own[...] += pick(side, part, half)
    msg[:, :half] = pick(side, part, half, other=True).astype(BF)
    msg[:, half:] = pieces(total)


def lower_kernel(
    kept, links, own, msg, msg_in, left_in, sum_other, acts, acts_in, vecs, vecs_in, dy,
    query, probs, left_keys, own_keys, dy_out, qg, key_own, leftward,
):
    tile, half = dy.shape
    side, _, keep_hi, keep_lo = where_am_i(kept, links)
    x = hi_of(side, acts, acts_in).astype(F32)
    inv = inverse_rms(x)
    left = left_in[...].astype(F32)
    x_mine = pick(side, x, half)
    gain = pick(side, hi_of(side, vecs, vecs_in)[:1], half)
    gate_lo = pick(side, lo_of(side, vecs, vecs_in)[1:2], half)
    total = unpieces(msg[:, half:]) + unpieces(msg_in[:, half:])
    total += jnp.sum(x_mine * gain * left, axis=-1, keepdims=True)
    total += sum_other[:, :1] / inv
    mean_term = total / x.shape[1]
    scaled = (own[...] + left + msg_in[:, :half].astype(F32)) * gain
    change = inv * (scaled - x_mine * inv * inv * mean_term)
    dy_old = dy[...]
    dy_new = jnp.where(keep_hi, (dy_old.astype(F32) + change).astype(BF), dy_old)
    dy_out[...] = dy_new
    grads = (gate_lo * dy_new.astype(F32)).astype(BF)
    for at in heads_of(half):
        keys = jnp.concatenate([left_keys[tile:, at], own_keys[tile:, at]], axis=0)
        start = at.start // HDIM * tile
        query_grad, key_grad = head_backward(query[:, at], keys, grads[:, at], probs[start : start + tile, :])
        qg[:, at] = jnp.where(keep_lo, query_grad, jnp.zeros_like(query_grad))
        leftward[:, at] = key_grad[:tile].astype(BF)
        key_own[:, at] = key_grad[tile:]


def project_kernel(kept, links, qg, weights, key_own, left_in, part_out, msg):
    half = qg.shape[1]
    side, _, _, _ = where_am_i(kept, links)
    part = mm(qg[...], weights[...], NT)
    mine = key_own[...] + left_in[...].astype(F32)
    first = part[:, :half] + jnp.where(side == 0, mine, 0.0)
    second = part[:, half:] + jnp.where(side == 1, mine, 0.0)
    part_out[:, :half] = first
    part_out[:, half:] = second
    msg[:, :half] = first.astype(BF)
    msg[:, half:] = second.astype(BF)


def finish_kernel(kept, links, part, msg_in, acts, acts_in, vecs, vecs_in, dy_mine, dy_in, out):
    side, _, _, keep_lo = where_am_i(kept, links)
    mine, other = dy_mine[...], dy_in[...]
    first = jnp.where(side == 0, mine, other)
    second = jnp.where(side == 0, other, mine)
    dy = jnp.concatenate([first, second], axis=1)
    x = lo_of(side, acts, acts_in).astype(F32)
    gain = lo_of(side, vecs, vecs_in)[:1]
    inv = inverse_rms(x)
    scaled = (part[...] + msg_in[...].astype(F32)) * gain
    mean_term = jnp.mean(x * scaled, axis=-1, keepdims=True)
    change = inv * (scaled - x * inv * inv * mean_term)
    updated = jnp.where(keep_lo, (dy.astype(F32) + change).astype(BF), dy)
    out[...] = jnp.where(side == 0, updated, dy)


def weight_grad_kernel(which, count, rows, kept, links, *refs):
    parts, grads, outs = refs[:count], refs[count : 2 * count], refs[2 * count :]
    fsdps = lax.axis_size("fsdp")
    fsdp = lax.axis_index("fsdp")
    block = parts[0].shape[0] // 2
    left = jnp.concatenate([p[which * block : (which + 1) * block, :] for p in parts], axis=1)
    right = jnp.concatenate([g[...] for g in grads], axis=0)
    scratch = outs[fsdps]
    scratch[...] = mm(left, right, NN).astype(BF)
    for shift in range(fsdps):
        source = pl.multiple_of(lax.rem(fsdp + shift, fsdps) * rows, rows)
        outs[shift][...] = scratch[pl.ds(source, rows), :]


def add_kernel(count, kept, links, *refs):
    hi_blocks, lo_blocks, (mine, theirs) = refs[:count], refs[count : 2 * count], refs[2 * count :]
    side, _, _, _ = where_am_i(kept, links)
    sums = []
    for blocks in (hi_blocks, lo_blocks):
        total = blocks[0][...].astype(F32)
        for block in blocks[1:]:
            total += block[...].astype(F32)
        sums.append(total.astype(BF))
    mine[...] = jnp.where(side == 1, sums[0], sums[1])
    theirs[...] = jnp.where(side == 1, sums[1], sums[0])


def tied(value, *others):
    return lax.optimization_barrier((value, *others))[0]


def per_device(acts, grad_out, gain, gate, w_query, kept, links):
    sections = lax.axis_size("section")
    fsdps = lax.axis_size("fsdp")
    seqs = lax.axis_size("seq")
    section_idx = lax.axis_index("section")
    seq_idx = lax.axis_index("seq")
    side = section_idx % 2
    tile, dim = acts.shape[2:]
    rows = w_query.shape[1]
    half = dim // 2
    swap_pairs = [(i, i ^ 1) for i in range(sections)]
    bits = [1 << b for b in reversed(range(seqs.bit_length() - 1))]
    offsets = [0]
    for bit in bits:
        offsets = offsets + [o ^ bit for o in offsets]

    def swap(value):
        return lax.ppermute(value, "section", swap_pairs)

    def across(value, offset):
        return lax.ppermute(value, "seq", [(s, s ^ offset) for s in range(seqs)])

    def along(value, shift):
        return lax.ppermute(value, "fsdp", [(f, (f + shift) % fsdps) for f in range(fsdps)])

    def run(kernel, outs, flops, name, *args, scratch=()):
        return call(kernel, outs, flops, name, kept, links, *args, scratch=scratch)

    first, second = w_query[0][:, :half], w_query[0][:, half:]
    w_own, w_theirs = jnp.where(side == 0, first, second), jnp.where(side == 0, second, first)
    w_other = swap(w_theirs)
    acts_own = acts[0, 0]
    acts_in = swap(acts_own)
    vecs = jnp.concatenate([gain, gate], axis=0)
    vecs_in = swap(vecs)
    top = bits[0]

    w_hi, w_lo = run(select_kernel, [sds((rows, half), BF)] * 2, rows * half, "select_w", w_own, w_other)
    matmul_flops = 2 * tile * dim * half
    head_flops = 2 * tile * 2 * tile * half
    part_shape = sds((2 * fsdps * rows, tile), BF)

    normalized = run(
        lambda *refs: normalize_kernel(offsets, rows, *refs),
        [sds((tile, dim), BF)] * 2 + [sds((2 * tile, half), BF)] + [part_shape] * seqs + [sds((tile, half), BF)],
        20 * tile * dim,
        "normalize",
        acts_own, acts_in, vecs, vecs_in, grad_out[0],
        scratch=[pltpu.VMEM((dim, tile), BF)],
    )
    normed_hi, normed_lo, keys = normalized[:3]
    parts = normalized[3 : 3 + seqs]
    incoming = normalized[-1]
    right_pairs = [(t, t + 1) for t in range(seqs - 1)]
    left_pairs = [(t + 1, t) for t in range(seqs - 1)]
    diagonal_pairs = [
        (s * seqs + t + 1, (s ^ 1) * seqs + t) for s in range(sections) for t in range(seqs - 1)
    ]
    left = lax.ppermute(keys, "seq", right_pairs)

    def over_fsdp(shard):
        return [shard] + [along(shard, shift) for shift in range(1, fsdps)]

    def over_seq(near, after=None):
        far = []
        for index, block in enumerate(near):
            if after is not None and index == fsdps - 1:
                block = tied(block, after)
            far.append(across(block, top))
        held = [(jnp.concatenate(near, axis=0), 0), (jnp.concatenate(far, axis=0), top)]
        for bit in bits[1:]:
            held = held + [(across(value, bit), offset ^ bit) for value, offset in held]
        places = [[(shift, offset) for shift in range(fsdps)] for _, offset in held]
        return far, [value for value, _ in held], places

    near_hi = over_fsdp(w_hi)
    _, blocks_hi, places = over_seq(near_hi, after=normed_hi)
    near_lo = over_fsdp(tied(w_lo, *near_hi[1:]))
    far_lo, blocks_lo, _ = over_seq(near_lo)

    def forward(name, which, normed, blocks):
        return run(
            lambda *refs: forward_kernel(which, places, rows, *refs),
            [sds((tile, half), BF), sds((half // HDIM * tile, 2 * tile), F32), sds((dim, half), BF)],
            matmul_flops + head_flops,
            name, normed, left, keys, *blocks,
        )

    query_hi, probs_hi, weights_hi = forward("forward_hi", 0, normed_hi, blocks_hi)
    query_lo, probs_lo, weights_lo = forward("forward_lo", 1, normed_lo, blocks_lo)

    parts_in = [parts[0]] + [
        across(tied(part, *far_lo), offset) for part, offset in zip(parts[1:], offsets[1:])
    ]

    kept_state = None
    for tick in range(sections // 2):
        qg_hi, own, msg, leftward, leftsum = run(
            upper_kernel,
            [
                sds((tile, half), BF),
                sds((tile, half), F32),
                sds((tile, half + HDIM), BF),
                sds((tile, half), BF),
                sds((tile, HDIM), F32),
            ],
            matmul_flops + 4 * head_flops,
            "upper", incoming, acts_own, acts_in, vecs, vecs_in, query_hi, probs_hi, weights_hi, left, keys,
        )
        msg_in = tied(swap(msg), *parts_in)
        left_in = lax.ppermute(leftward, "seq", left_pairs)
        sum_other = lax.ppermute(leftsum, ("section", "seq"), diagonal_pairs)
        dy_mid, qg_lo, key_own, leftward_lo = run(
            lower_kernel,
            [sds((tile, half), BF), sds((tile, half), BF), sds((tile, half), F32), sds((tile, half), BF)],
            4 * head_flops,
            "lower",
            own, msg, msg_in, left_in, sum_other, acts_own, acts_in, vecs, vecs_in, incoming,
            query_lo, probs_lo, left, keys,
        )
        left_in_lo = lax.ppermute(leftward_lo, "seq", left_pairs)
        dy_in = swap(dy_mid)
        part_lo, msg_lo = run(
            project_kernel, [sds((tile, dim), F32), sds((tile, dim), BF)], matmul_flops, "project_lo",
            qg_lo, weights_lo, key_own, left_in_lo,
        )
        msg_lo_in = lax.ppermute(msg_lo, "section", [(i + 1, i) for i in range(0, sections, 2)])
        (updated,) = run(
            finish_kernel, [sds((tile, dim), BF)], 20 * tile * dim, "finish",
            part_lo, msg_lo_in, acts_own, acts_in, vecs, vecs_in, dy_mid, dy_in,
        )
        state = (updated, qg_hi, qg_lo)
        if kept_state is None:
            kept_state = state
        else:
            active = section_idx // 2 == sections // 2 - 1 - tick
            kept_state = jax.tree.map(lambda new, old: jnp.where(active, new, old), state, kept_state)
        if tick + 1 < sections // 2:
            to_low = lax.ppermute(updated[:, :half], "section", [(i, i - 2) for i in range(2, sections, 2)])
            to_high = lax.ppermute(updated[:, half:], "section", [(i, i - 1) for i in range(2, sections, 2)])
            incoming = jnp.where(side == 0, to_low, to_high)
    result, qg_hi, qg_lo = kept_state

    def weight_grad(name, which, query_grad, after):
        gathered = [query_grad]
        for bit in bits:
            arrived = across(jnp.concatenate(gathered, axis=0) if len(gathered) > 1 else gathered[0], bit)
            gathered = gathered + [arrived[i * tile : (i + 1) * tile] for i in range(len(gathered))]
        if after is not None:
            gathered[-1] = tied(gathered[-1], after)
        terms = run(
            lambda *refs: weight_grad_kernel(which, seqs, rows, *refs),
            [sds((rows, half), BF)] * fsdps,
            2 * fsdps * rows * seqs * tile * half,
            name, *parts_in, *gathered,
            scratch=[pltpu.VMEM((fsdps * rows, half), BF)],
        )
        return [terms[0]] + [along(terms[shift], shift) for shift in range(1, fsdps)]

    terms_hi = weight_grad("weight_grad_hi", 0, qg_hi, qg_lo)
    terms_lo = weight_grad("weight_grad_lo", 1, qg_lo, None)
    terms_lo[-1] = tied(terms_lo[-1], result)
    mine, theirs = run(
        lambda *refs: add_kernel(fsdps, *refs),
        [sds((rows, half), BF)] * 2, 20 * rows * half, "add_clips", *terms_hi, *terms_lo,
    )
    other = swap(theirs)
    first = jnp.where(side == 0, mine, other)
    second = jnp.where(side == 0, other, mine)
    grad_rows = jnp.concatenate([first, second], axis=1)
    return (result[None, None], grad_rows[None])


def solution(mesh):
    placed = (
        P("section", "fsdp", "seq", None),
        P("fsdp", "seq", None),
        P("section", None),
        P("section", None),
        P("section", ("fsdp", "seq"), None),
        P("fsdp", None),
        P("fsdp", "seq"),
    )
    return jax.shard_map(
        per_device,
        mesh=mesh,
        in_specs=placed,
        out_specs=(P("section", "fsdp", "seq", None), P("section", ("fsdp", "seq"), None)),
        check_vma=False,
    )
```

```python
import jax
import jax.numpy as jnp
from jax import lax
from jax.experimental import pallas as pl
from jax.experimental.pallas import tpu as pltpu
from jax.sharding import PartitionSpec as P

HDIM = 128
SCALE = HDIM ** (-0.5)
EPS = 1e-06
NEG = -1e30
BF = jnp.bfloat16
F32 = jnp.float32
VLIMIT = 16 * 1024 * 1024

NN = (((1,), (0,)), ((), ()))
NT = (((1,), (1,)), ((), ()))
TN = (((0,), (0,)), ((), ()))


def mm(a, b, dims):
    return lax.dot_general(a, b, dims, preferred_element_type=F32)


def sds(shape, dtype):
    return jax.ShapeDtypeStruct(shape, dtype)


def call(kernel, outs, flops, name, *args, scalars=(), scratch=()):
    nbytes = sum(s.size * s.dtype.itemsize for s in outs) + sum(a.size * a.dtype.itemsize for a in args)
    return pl.pallas_call(
        kernel,
        out_shape=outs,
        in_specs=[pl.BlockSpec(memory_space=pltpu.SMEM)] * len(scalars)
        + [pl.BlockSpec(memory_space=pltpu.VMEM)] * len(args),
        out_specs=[pl.BlockSpec(memory_space=pltpu.VMEM)] * len(outs),
        scratch_shapes=list(scratch),
        compiler_params=pltpu.CompilerParams(vmem_limit_bytes=VLIMIT),
        cost_estimate=pl.CostEstimate(flops=flops, bytes_accessed=nbytes, transcendentals=0),
        name=name,
    )(*scalars, *args)


def my_side():
    return lax.rem(lax.axis_index("section"), 2)


def is_kept(kept, section_hi):
    hi = lax.axis_index("section") - my_side() + 1
    return kept[0, hi if section_hi else hi - 1] > 0


def pick(side, value, half, other=False):
    first = value[:, :half]
    second = value[:, half:]
    use_first = (side == 1) if other else (side == 0)
    return jnp.where(use_first, first, second)


def inverse_rms(x):
    return lax.rsqrt(jnp.mean(x * x, axis=-1, keepdims=True) + EPS)


def three_terms(value):
    high = value.astype(BF)
    rest = value - high.astype(F32)
    middle = rest.astype(BF)
    return high, middle, (rest - middle.astype(F32)).astype(BF)


def pack_kernel(acts, gain, gate, packed):
    tile = acts.shape[0]
    packed[:tile, :] = acts[...]
    shape = (packed.shape[0] - tile, acts.shape[1])
    row = lax.broadcasted_iota(jnp.int32, shape, 0)
    terms = jnp.zeros(shape, F32)
    for index, term in enumerate(three_terms(gain[...]) + three_terms(gate[...])):
        terms = jnp.where(row == index, jnp.broadcast_to(term.astype(F32), shape), terms)
    packed[tile:, :] = terms.astype(BF)


def select_kernel(own, other, hi, lo):
    side = my_side()
    hi[...] = jnp.where(side == 1, own[...], other[...])
    lo[...] = jnp.where(side == 1, other[...], own[...])


def row_blocks(value, offsets, rows, parts, turned):
    seqs = len(offsets)
    block = parts[0].shape[0] // (seqs // 2)
    seq = lax.axis_index("seq")
    turned[...] = value.astype(F32).T.astype(BF)
    for offset in offsets:
        part = parts[0] if offset < seqs // 2 else parts[1]
        base = offset % (seqs // 2) * block
        for f in range(block // rows):
            source = pl.multiple_of((f * seqs + jnp.bitwise_xor(seq, offset)) * rows, rows)
            part[base + f * rows : base + (f + 1) * rows, :] = turned[pl.ds(source, rows), :]


def normalize_own_kernel(offsets, rows, acts, gain, normed, low, high, turned):
    x = acts[...].astype(F32)
    value = (x * inverse_rms(x) * gain[...]).astype(BF)
    normed[...] = value
    row_blocks(value, offsets, rows, (low, high), turned)


def normalize_kernel(acts, packed, gain, gate, dy_full, normed_own, *outs):
    xs, normed, (keys, vecs, dy) = outs[:2], outs[2:4], outs[4:]
    tile, half = dy.shape
    extra = packed[tile:, :].astype(F32)
    gain_in = extra[0:1] + extra[1:2] + extra[2:3]
    gate_in = extra[3:4] + extra[4:5] + extra[5:6]
    x = packed[:tile, :].astype(F32)
    value = (x * inverse_rms(x) * gain_in).astype(BF)
    own = acts[...], normed_own[...], gain[...], gate[...]
    other = packed[:tile, :], value, gain_in, gate_in
    side = my_side()
    for which in range(2):
        take_own = side == 1 - which
        x_low, rounded, gain_row, gate_row = [jnp.where(take_own, a, b) for a, b in zip(own, other)]
        xs[which][...] = x_low
        normed[which][...] = rounded
        vecs[2 * which : 2 * which + 1, :] = gain_row
        vecs[2 * which + 1 : 2 * which + 2, :] = gate_row
        keys[which * tile : (which + 1) * tile, :] = pick(side, rounded, half)
    dy[...] = pick(side, dy_full[...], half)


def head_probs(query, keys, linked):
    scores = mm(query, keys, NT) * SCALE
    column = lax.broadcasted_iota(jnp.int32, scores.shape, 1)
    scores = jnp.where(jnp.logical_or(column >= scores.shape[1] // 2, linked), scores, NEG)
    exps = jnp.exp(scores - jnp.max(scores, axis=-1, keepdims=True))
    return exps / jnp.sum(exps, axis=-1, keepdims=True)


def head_backward(query, keys, grads, probs):
    prob_grad = mm(grads, keys, NT)
    row_delta = jnp.sum(probs * prob_grad, axis=-1, keepdims=True)
    score_grad = (probs * (prob_grad - row_delta) * SCALE).astype(BF)
    query_grad = mm(score_grad, keys, NN).astype(BF)
    key_grad = mm(
        jnp.concatenate([score_grad, probs.astype(BF)], axis=0),
        jnp.concatenate([query, grads], axis=0),
        TN,
    )
    return query_grad, key_grad


def pieces(column):
    rows = column.shape[0]
    lane = lax.broadcasted_iota(jnp.int32, (rows, HDIM), 1)
    high, middle, low = [jnp.broadcast_to(p.astype(F32), (rows, HDIM)) for p in three_terms(column)]
    value = jnp.where(lane == 0, high, jnp.where(lane == 1, middle, jnp.where(lane == 2, low, 0.0)))
    return value.astype(BF)


def unpieces(block):
    return jnp.sum(block.astype(F32), axis=-1, keepdims=True)


def heads_of(half):
    return [slice(h * HDIM, (h + 1) * HDIM) for h in range(half // HDIM)]


def pairs_of(half):
    step = 2 * HDIM if half % (2 * HDIM) == 0 else HDIM
    return [slice(c, c + step) for c in range(0, half, step)]


def forward_kernel(which, places, rows, links, normed, left_keys, own_keys, *rest):
    blocks = rest[: len(places)]
    query_out, probs_out, weights = rest[len(places) :]
    tile, half = query_out.shape
    token = slice(which * tile, (which + 1) * tile)
    seqs = lax.axis_size("seq")
    fsdp, seq = lax.axis_index("fsdp"), lax.axis_index("seq")
    linked = jnp.logical_and(links[0, 0] > 0, seq > 0)
    for block, place in zip(blocks, places):
        for index, (flip, offset) in enumerate(place):
            f = jnp.bitwise_xor(fsdp, flip)
            target = pl.multiple_of((f * seqs + jnp.bitwise_xor(seq, offset)) * rows, rows)
            weights[pl.ds(target, rows), :] = block[index * rows : (index + 1) * rows, :]
    tokens = normed[...]
    for cols in pairs_of(half):
        query = mm(tokens, weights[:, cols], NN).astype(BF)
        query_out[:, cols] = query
        for sub in heads_of(cols.stop - cols.start):
            at = slice(cols.start + sub.start, cols.start + sub.stop)
            keys = jnp.concatenate([left_keys[token, at], own_keys[token, at]], axis=0)
            start = at.start // HDIM * tile
            probs_out[start : start + tile, :] = head_probs(query[:, sub], keys, linked)


def upper_kernel(
    kept, dy, acts, vecs, query, probs, weights, left_keys, own_keys, qg, own, msg, leftward, leftsum
):
    tile, half = dy.shape
    side = my_side()
    keep = is_kept(kept, True)
    gate = pick(side, vecs[1:2, :], half)
    grads = (gate * dy[...].astype(F32)).astype(BF)
    left_total = jnp.zeros((tile, 1), F32)
    for at in heads_of(half):
        left = left_keys[:tile, at]
        keys = jnp.concatenate([left, own_keys[:tile, at]], axis=0)
        start = at.start // HDIM * tile
        query_grad, key_grad = head_backward(query[:, at], keys, grads[:, at], probs[start : start + tile, :])
        qg[:, at] = jnp.where(keep, query_grad, jnp.zeros_like(query_grad))
        back = key_grad[:tile].astype(BF)
        leftward[:, at] = back
        left_total += jnp.sum(back.astype(F32) * left.astype(F32), axis=-1, keepdims=True)
        own[:, at] = key_grad[tile:]
    leftsum[...] = jnp.broadcast_to(left_total, leftsum.shape)
    part = mm(qg[...], weights[...], NT)
    x_gain = acts[...].astype(F32) * vecs[:1, :]
    total = jnp.sum(x_gain * part, axis=-1, keepdims=True)
    total += jnp.sum(pick(side, x_gain, half) * own[...], axis=-1, keepdims=True)
    own[...] += pick(side, part, half)
    msg[:, :half] = pick(side, part, half, other=True).astype(BF)
    msg[:, half:] = pieces(total)


def lower_kernel(
    kept, own, msg, msg_in, left_in, sum_other, acts, vecs, dy, query, probs, left_keys, own_keys,
    dy_out, qg, key_own, leftward,
):
    tile, half = dy.shape
    side = my_side()
    keep_hi, keep_lo = is_kept(kept, True), is_kept(kept, False)
    x = acts[...].astype(F32)
    inv = inverse_rms(x)
    left = left_in[...].astype(F32)
    x_mine = pick(side, x, half)
    gain = pick(side, vecs[:1, :], half)
    gate_lo = pick(side, vecs[3:4, :], half)
    total = unpieces(msg[:, half:]) + unpieces(msg_in[:, half:])
    total += jnp.sum(x_mine * gain * left, axis=-1, keepdims=True)
    total += sum_other[:, :1] / inv
    mean_term = total / x.shape[1]
    scaled = (own[...] + left + msg_in[:, :half].astype(F32)) * gain
    change = inv * (scaled - x_mine * inv * inv * mean_term)
    dy_old = dy[...]
    dy_new = jnp.where(keep_hi, (dy_old.astype(F32) + change).astype(BF), dy_old)
    dy_out[...] = dy_new
    grads = (gate_lo * dy_new.astype(F32)).astype(BF)
    for at in heads_of(half):
        keys = jnp.concatenate([left_keys[tile:, at], own_keys[tile:, at]], axis=0)
        start = at.start // HDIM * tile
        query_grad, key_grad = head_backward(query[:, at], keys, grads[:, at], probs[start : start + tile, :])
        qg[:, at] = jnp.where(keep_lo, query_grad, jnp.zeros_like(query_grad))
        leftward[:, at] = key_grad[:tile].astype(BF)
        key_own[:, at] = key_grad[tile:]


def project_kernel(qg, weights, key_own, left_in, dy, part_out, msg):
    half = qg.shape[1]
    side = my_side()
    part = mm(qg[...], weights[...], NT)
    mine = key_own[...] + left_in[...].astype(F32)
    first = part[:, :half] + jnp.where(side == 0, mine, 0.0)
    second = part[:, half:] + jnp.where(side == 1, mine, 0.0)
    part_out[:, :half] = first
    part_out[:, half:] = second
    msg[:, :half] = first.astype(BF)
    msg[:, half : 2 * half] = second.astype(BF)
    msg[:, 2 * half :] = dy[...]


def finish_kernel(kept, part, msg_in, acts, vecs, dy_mine, out):
    half = dy_mine.shape[1]
    side = my_side()
    mine, other = dy_mine[...], msg_in[:, 2 * half :]
    first = jnp.where(side == 0, mine, other)
    second = jnp.where(side == 0, other, mine)
    dy = jnp.concatenate([first, second], axis=1)
    x = acts[...].astype(F32)
    inv = inverse_rms(x)
    scaled = (part[...] + msg_in[:, : 2 * half].astype(F32)) * vecs[2:3, :]
    mean_term = jnp.mean(x * scaled, axis=-1, keepdims=True)
    change = inv * (scaled - x * inv * inv * mean_term)
    updated = jnp.where(is_kept(kept, False), (dy.astype(F32) + change).astype(BF), dy)
    out[...] = jnp.where(side == 0, updated, dy)


def weight_grad_kernel(section_hi, flips, rows, own, other, *refs):
    grads, (kept_rows, sent_rows, scratch) = refs[:-3], refs[-3:]
    fsdp = lax.axis_index("fsdp")
    block = scratch.shape[0]
    take_own = (my_side() == 1) if section_hi else (my_side() == 0)
    parts = jnp.where(take_own, own[...], other[...])
    left = jnp.concatenate([parts[i : i + block] for i in range(0, parts.shape[0], block)], axis=1)
    right = jnp.concatenate([g[...] for g in grads], axis=0)
    scratch[...] = mm(left, right, NN).astype(BF)
    count = len(flips) // 2
    for index, flip in enumerate(flips):
        source = pl.multiple_of(jnp.bitwise_xor(fsdp, flip) * rows, rows)
        out = kept_rows if index < count else sent_rows
        target = index % count * rows
        out[target : target + rows, :] = scratch[pl.ds(source, rows), :]


def add_halves_kernel(kept_rows, arrived, mine, sent):
    total = (kept_rows[...].astype(F32) + arrived[...].astype(F32)).astype(BF)
    count = mine.shape[0]
    mine[...] = total[:count]
    sent[...] = total[count:]


def add_kernel(hi_mine, hi_arrived, lo_mine, lo_arrived, mine, theirs):
    side = my_side()
    grad_hi = (hi_mine[...].astype(F32) + hi_arrived[...].astype(F32)).astype(BF)
    grad_lo = (lo_mine[...].astype(F32) + lo_arrived[...].astype(F32)).astype(BF)
    mine[...] = jnp.where(side == 1, grad_hi, grad_lo)
    theirs[...] = jnp.where(side == 1, grad_lo, grad_hi)


def tied(value, *others):
    return lax.optimization_barrier((value, *others))[0]


def per_device(acts, grad_out, gain, gate, w_query, kept, links):
    sections = lax.axis_size("section")
    fsdps = lax.axis_size("fsdp")
    seqs = lax.axis_size("seq")
    section_idx = lax.axis_index("section")
    side = section_idx % 2
    tile, dim = acts.shape[2:]
    rows = w_query.shape[1]
    half = dim // 2
    swap_pairs = [(i, i ^ 1) for i in range(sections)]
    bits = [1 << b for b in reversed(range(seqs.bit_length() - 1))]
    top = bits[0]
    steps = [1 << b for b in reversed(range(fsdps.bit_length() - 1))]
    flips = [0]
    for step in steps:
        flips = flips + [f ^ step for f in flips]
    owners = [0]
    for step in steps:
        owners = owners + [f ^ step for f in owners]
    offsets = list(range(seqs))
    right_pairs = [(t, t + 1) for t in range(seqs - 1)]
    left_pairs = [(t + 1, t) for t in range(seqs - 1)]
    diagonal_pairs = [
        (s * seqs + t + 1, (s ^ 1) * seqs + t) for s in range(sections) for t in range(seqs - 1)
    ]
    matmul_flops = 2 * tile * dim * half
    head_flops = 2 * tile * 2 * tile * half

    def swap(value):
        return lax.ppermute(value, "section", swap_pairs)

    def across(value, offset):
        return lax.ppermute(value, "seq", [(s, s ^ offset) for s in range(seqs)])

    def along(value, flip):
        return lax.ppermute(value, "fsdp", [(f, f ^ flip) for f in range(fsdps)])

    def join(values):
        return values[0] if len(values) == 1 else jnp.concatenate(values, axis=0)

    acts_own = acts[0, 0]
    first, second = w_query[0][:, :half], w_query[0][:, half:]
    w_own, w_theirs = jnp.where(side == 0, first, second), jnp.where(side == 0, second, first)
    w_other = swap(w_theirs)
    (packed,) = call(
        pack_kernel, [sds((tile + 16, dim), BF)], 10 * tile * dim, "pack", acts_own, gain, gate
    )
    packed_in = swap(packed)

    unit = fsdps * rows
    part_shapes = [sds((seqs // 2 * unit, tile), BF)] * 2
    turned = pltpu.VMEM((dim, tile), BF)

    def to_row_owners(low, high):
        parts = [(low, [0]), (across(high, top), [0])]
        for bit in bits[1:]:
            sent = [v[b + bit * unit : b + 2 * bit * unit] for v, begins in parts for b in begins]
            arrived = across(join(sent), bit)
            parts = parts + [(arrived, [i * bit * unit for i in range(len(sent))])]
        return join([v[b : b + unit] for v, begins in parts for b in begins])

    normed_own, low_own, high_own = call(
        lambda *refs: normalize_own_kernel(offsets, rows, *refs),
        [sds((tile, dim), BF)] + part_shapes, 20 * tile * dim,
        "normalize_own", acts_own, gain, scratch=[turned],
    )
    w_hi, w_lo = call(
        select_kernel, [sds((rows, half), BF)] * 2, rows * half,
        "select_w", w_own, tied(w_other, packed, high_own),
    )
    parts_own = to_row_owners(low_own, high_own)
    def over_fsdp(shard):
        near = [shard]
        for step in steps:
            near = near + [along(join(near), step)]
        return near

    def over_seq(near, after=(), after_last=()):
        sent = [join(near[:2])] + near[2:]
        if after:
            sent = [tied(value, *after) for value in sent]
        if after_last:
            sent[-1] = tied(sent[-1], *after_last)
        return [across(value, top) for value in sent]

    def between_cores(near, far, after=()):
        if after:
            far = [tied(value, *after) for value in far]
        held = [join(near + far)]
        places = [[(f, 0) for f in flips] + [(f, top) for f in flips]]
        for bit in bits[1:]:
            held = held + [across(v, bit) for v in held]
            places = places + [[(f, o ^ bit) for f, o in place] for place in places]
        return held, places

    near_hi = over_fsdp(w_hi)
    far_hi = over_seq(near_hi, after_last=[packed_in, parts_own])
    x_hi, x_lo, normed_hi, normed_lo, keys, vecs, incoming = call(
        normalize_kernel,
        [sds((tile, dim), BF)] * 4 + [sds((2 * tile, half), BF), sds((8, dim), F32), sds((tile, half), BF)],
        30 * tile * dim,
        "normalize", acts_own, packed_in, gain, gate, grad_out[0], tied(normed_own, far_hi[0]),
    )
    left = lax.ppermute(keys, "seq", right_pairs)
    near_lo = over_fsdp(tied(w_lo, near_hi[1], packed_in))
    blocks_hi, places = between_cores(near_hi, far_hi, after=[near_lo[-1], left])
    far_lo = over_seq(near_lo, after=[left])

    def forward(name, which, normed, blocks):
        return call(
            lambda *refs: forward_kernel(which, places, rows, *refs),
            [sds((tile, half), BF), sds((half // HDIM * tile, 2 * tile), F32), sds((dim, half), BF)],
            matmul_flops + head_flops,
            name, normed, left, keys, *blocks, scalars=[links],
        )

    query_hi, probs_hi, weights_hi = forward("forward_hi", 0, normed_hi, blocks_hi)
    def over_tiles(query_grad):
        gathered = [query_grad]
        for bit in bits:
            gathered = gathered + [across(join(gathered), bit)]
        return gathered

    def weight_grad(name, section_hi, gathered):
        halves = [sds((fsdps // 2 * rows, half), BF)] * 2
        return call(
            lambda *refs: weight_grad_kernel(section_hi, owners, rows, *refs),
            halves,
            2 * fsdps * rows * seqs * tile * half,
            name, parts_own, parts_other, *gathered,
            scratch=[pltpu.VMEM((fsdps * rows, half), BF)],
        )

    def over_clips(name, mine, sent):
        arrived = along(sent, steps[-1])
        for step in reversed(steps[:-1]):
            count = mine.shape[0] // 2
            mine, sent = call(
                add_halves_kernel, [sds((count, half), BF)] * 2, 4 * count * half, name, mine, arrived
            )
            arrived = along(sent, step)
        return mine, arrived

    kept_state = None
    single = sections == 2
    for tick in range(sections // 2):
        qg_hi, own, msg, leftward, leftsum = call(
            upper_kernel,
            [
                sds((tile, half), BF),
                sds((tile, half), F32),
                sds((tile, half + HDIM), BF),
                sds((tile, half), BF),
                sds((tile, HDIM), F32),
            ],
            matmul_flops + 4 * head_flops,
            "upper", incoming, x_hi, vecs, query_hi, probs_hi, weights_hi, left, keys, scalars=[kept],
        )
        msg_in = swap(msg)
        left_in = lax.ppermute(leftward, "seq", left_pairs)
        sum_other = lax.ppermute(leftsum, ("section", "seq"), diagonal_pairs)
        exchanged = [msg_in, left_in, sum_other]
        if tick == 0:
            parts_other = swap(tied(parts_own, msg_in))
            blocks_lo, _ = between_cores(near_lo, far_lo, after=exchanged)
            query_lo, probs_lo, weights_lo = forward("forward_lo", 1, normed_lo, blocks_lo)
        dy_mid, qg_lo, key_own, leftward_lo = call(
            lower_kernel,
            [sds((tile, half), BF), sds((tile, half), BF), sds((tile, half), F32), sds((tile, half), BF)],
            4 * head_flops,
            "lower", own, msg, msg_in, left_in, sum_other, x_hi, vecs, incoming,
            query_lo, probs_lo, left, keys, scalars=[kept],
        )
        left_in_lo = lax.ppermute(leftward_lo, "seq", left_pairs)
        if single:
            gathered_hi = over_tiles(tied(qg_hi, *exchanged))
            gathered_hi[-1] = tied(gathered_hi[-1], qg_lo)
            clips_hi = over_clips("add_pair_hi", *weight_grad("weight_grad_hi", True, gathered_hi))
            clips_lo = over_clips("add_pair_lo", *weight_grad("weight_grad_lo", False, over_tiles(qg_lo)))
            left_in_lo = tied(left_in_lo, clips_hi[0])
        part_lo, msg_lo = call(
            project_kernel, [sds((tile, dim), F32), sds((tile, dim + half), BF)], matmul_flops,
            "project_lo", qg_lo, weights_lo, key_own, left_in_lo, dy_mid,
        )
        msg_lo_in = swap(msg_lo)
        (updated,) = call(
            finish_kernel, [sds((tile, dim), BF)], 20 * tile * dim,
            "finish", part_lo, msg_lo_in, x_lo, vecs, dy_mid, scalars=[kept],
        )
        state = (updated, qg_hi, qg_lo)
        if kept_state is None:
            kept_state = state
        else:
            active = section_idx // 2 == sections // 2 - 1 - tick
            kept_state = jax.tree.map(lambda new, old: jnp.where(active, new, old), state, kept_state)
        if tick + 1 < sections // 2:
            to_low = lax.ppermute(updated[:, :half], "section", [(i, i - 2) for i in range(2, sections, 2)])
            to_high = lax.ppermute(updated[:, half:], "section", [(i, i - 1) for i in range(2, sections, 2)])
            incoming = jnp.where(side == 0, to_low, to_high)
    result, qg_hi, qg_lo = kept_state
    if not single:
        clips_hi = over_clips("add_pair_hi", *weight_grad("weight_grad_hi", True, over_tiles(qg_hi)))
        clips_lo = over_clips("add_pair_lo", *weight_grad("weight_grad_lo", False, over_tiles(qg_lo)))

    mine, theirs = call(
        add_kernel, [sds((rows, half), BF)] * 2, 20 * rows * half,
        "add_clips", *clips_hi, clips_lo[0], tied(clips_lo[1], result),
    )
    other = swap(theirs)
    first = jnp.where(side == 0, mine, other)
    second = jnp.where(side == 0, other, mine)
    grad_rows = jnp.concatenate([first, second], axis=1)
    return (result[None, None], grad_rows[None])


def solution(mesh):
    placed = (
        P("section", "fsdp", "seq", None),
        P("fsdp", "seq", None),
        P("section", None),
        P("section", None),
        P("section", ("fsdp", "seq"), None),
        P("fsdp", None),
        P("fsdp", "seq"),
    )
    return jax.shard_map(
        per_device,
        mesh=mesh,
        in_specs=placed,
        out_specs=(P("section", "fsdp", "seq", None), P("section", ("fsdp", "seq"), None)),
        check_vma=False,
    )
```

```python
import jax
import jax.numpy as jnp
from jax import lax
from jax.experimental import pallas as pl
from jax.experimental.pallas import tpu as pltpu
from jax.sharding import PartitionSpec as P

HDIM = 128
SCALE = HDIM ** (-0.5)
EPS = 1e-06
NEG = -1e30
BF = jnp.bfloat16
F32 = jnp.float32
VLIMIT = 16 * 1024 * 1024

NN = (((1,), (0,)), ((), ()))
NT = (((1,), (1,)), ((), ()))
TN = (((0,), (0,)), ((), ()))


def mm(a, b, dims):
    return lax.dot_general(a, b, dims, preferred_element_type=F32)


def sds(shape, dtype):
    return jax.ShapeDtypeStruct(shape, dtype)


def call(kernel, outs, flops, name, *args, scalars=(), scratch=()):
    nbytes = sum(s.size * s.dtype.itemsize for s in outs) + sum(a.size * a.dtype.itemsize for a in args)
    return pl.pallas_call(
        kernel,
        out_shape=outs,
        in_specs=[pl.BlockSpec(memory_space=pltpu.SMEM)] * len(scalars)
        + [pl.BlockSpec(memory_space=pltpu.VMEM)] * len(args),
        out_specs=[pl.BlockSpec(memory_space=pltpu.VMEM)] * len(outs),
        scratch_shapes=list(scratch),
        compiler_params=pltpu.CompilerParams(vmem_limit_bytes=VLIMIT),
        cost_estimate=pl.CostEstimate(flops=flops, bytes_accessed=nbytes, transcendentals=0),
        name=name,
    )(*scalars, *args)


def my_side():
    return lax.rem(lax.axis_index("section"), 2)


def is_kept(kept, section_hi):
    hi = lax.axis_index("section") - my_side() + 1
    return kept[0, hi if section_hi else hi - 1] > 0


def pick(side, value, half, other=False):
    first = value[:, :half]
    second = value[:, half:]
    use_first = (side == 1) if other else (side == 0)
    return jnp.where(use_first, first, second)


def inverse_rms(x):
    return lax.rsqrt(jnp.mean(x * x, axis=-1, keepdims=True) + EPS)


def three_terms(value):
    high = value.astype(BF)
    rest = value - high.astype(F32)
    middle = rest.astype(BF)
    return high, middle, (rest - middle.astype(F32)).astype(BF)


def pack_kernel(acts, gain, gate, packed):
    tile = acts.shape[0]
    packed[:tile, :] = acts[...]
    shape = (packed.shape[0] - tile, acts.shape[1])
    row = lax.broadcasted_iota(jnp.int32, shape, 0)
    terms = jnp.zeros(shape, F32)
    for index, term in enumerate(three_terms(gain[...]) + three_terms(gate[...])):
        terms = jnp.where(row == index, jnp.broadcast_to(term.astype(F32), shape), terms)
    packed[tile:, :] = terms.astype(BF)


def select_kernel(own, other, hi, lo):
    side = my_side()
    hi[...] = jnp.where(side == 1, own[...], other[...])
    lo[...] = jnp.where(side == 1, other[...], own[...])


def row_blocks(value, offsets, rows, parts, turned):
    seqs = len(offsets)
    block = parts[0].shape[0] // (seqs // 2)
    seq = lax.axis_index("seq")
    turned[...] = value.astype(F32).T.astype(BF)
    for offset in offsets:
        part = parts[0] if offset < seqs // 2 else parts[1]
        base = offset % (seqs // 2) * block
        for f in range(block // rows):
            source = pl.multiple_of((f * seqs + jnp.bitwise_xor(seq, offset)) * rows, rows)
            part[base + f * rows : base + (f + 1) * rows, :] = turned[pl.ds(source, rows), :]


def normalize_own_kernel(offsets, rows, acts, gain, normed, low, high, turned):
    x = acts[...].astype(F32)
    value = (x * inverse_rms(x) * gain[...]).astype(BF)
    normed[...] = value
    row_blocks(value, offsets, rows, (low, high), turned)


def normalize_kernel(acts, packed, gain, gate, dy_full, normed_own, *outs):
    xs, normed, (keys, vecs, dy) = outs[:2], outs[2:4], outs[4:]
    tile, half = dy.shape
    extra = packed[tile:, :].astype(F32)
    gain_in = extra[0:1] + extra[1:2] + extra[2:3]
    gate_in = extra[3:4] + extra[4:5] + extra[5:6]
    x = packed[:tile, :].astype(F32)
    value = (x * inverse_rms(x) * gain_in).astype(BF)
    own = acts[...], normed_own[...], gain[...], gate[...]
    other = packed[:tile, :], value, gain_in, gate_in
    side = my_side()
    for which in range(2):
        take_own = side == 1 - which
        x_low, rounded, gain_row, gate_row = [jnp.where(take_own, a, b) for a, b in zip(own, other)]
        xs[which][...] = x_low
        normed[which][...] = rounded
        vecs[2 * which : 2 * which + 1, :] = gain_row
        vecs[2 * which + 1 : 2 * which + 2, :] = gate_row
        keys[which * tile : (which + 1) * tile, :] = pick(side, rounded, half)
    dy[...] = pick(side, dy_full[...], half)


def head_probs(query, keys, linked):
    scores = mm(query, keys, NT) * SCALE
    column = lax.broadcasted_iota(jnp.int32, scores.shape, 1)
    scores = jnp.where(jnp.logical_or(column >= scores.shape[1] // 2, linked), scores, NEG)
    exps = jnp.exp(scores - jnp.max(scores, axis=-1, keepdims=True))
    return exps / jnp.sum(exps, axis=-1, keepdims=True)


def head_backward(query, keys, grads, probs):
    prob_grad = mm(grads, keys, NT)
    row_delta = jnp.sum(probs * prob_grad, axis=-1, keepdims=True)
    score_grad = (probs * (prob_grad - row_delta) * SCALE).astype(BF)
    query_grad = mm(score_grad, keys, NN).astype(BF)
    key_grad = mm(
        jnp.concatenate([score_grad, probs.astype(BF)], axis=0),
        jnp.concatenate([query, grads], axis=0),
        TN,
    )
    return query_grad, key_grad


def pieces(column):
    rows = column.shape[0]
    lane = lax.broadcasted_iota(jnp.int32, (rows, HDIM), 1)
    high, middle, low = [jnp.broadcast_to(p.astype(F32), (rows, HDIM)) for p in three_terms(column)]
    value = jnp.where(lane == 0, high, jnp.where(lane == 1, middle, jnp.where(lane == 2, low, 0.0)))
    return value.astype(BF)


def unpieces(block):
    return jnp.sum(block.astype(F32), axis=-1, keepdims=True)


def heads_of(half):
    return [slice(h * HDIM, (h + 1) * HDIM) for h in range(half // HDIM)]


def pairs_of(half):
    step = 2 * HDIM if half % (2 * HDIM) == 0 else HDIM
    return [slice(c, c + step) for c in range(0, half, step)]


def forward_kernel(which, places, rows, links, normed, left_keys, own_keys, *rest):
    blocks = rest[: len(places)]
    query_out, probs_out, weights = rest[len(places) :]
    tile, half = query_out.shape
    token = slice(which * tile, (which + 1) * tile)
    seqs = lax.axis_size("seq")
    fsdp, seq = lax.axis_index("fsdp"), lax.axis_index("seq")
    linked = jnp.logical_and(links[0, 0] > 0, seq > 0)
    for block, place in zip(blocks, places):
        for index, (flip, offset) in enumerate(place):
            f = jnp.bitwise_xor(fsdp, flip)
            target = pl.multiple_of((f * seqs + jnp.bitwise_xor(seq, offset)) * rows, rows)
            weights[pl.ds(target, rows), :] = block[index * rows : (index + 1) * rows, :]
    tokens = normed[...]
    for cols in pairs_of(half):
        query = mm(tokens, weights[:, cols], NN).astype(BF)
        query_out[:, cols] = query
        for sub in heads_of(cols.stop - cols.start):
            at = slice(cols.start + sub.start, cols.start + sub.stop)
            keys = jnp.concatenate([left_keys[token, at], own_keys[token, at]], axis=0)
            start = at.start // HDIM * tile
            probs_out[start : start + tile, :] = head_probs(query[:, sub], keys, linked)


def upper_kernel(
    kept, dy, acts, vecs, query, probs, weights, left_keys, own_keys, qg, own, msg, leftward, leftsum
):
    tile, half = dy.shape
    side = my_side()
    keep = is_kept(kept, True)
    gate = pick(side, vecs[1:2, :], half)
    grads = (gate * dy[...].astype(F32)).astype(BF)
    left_total = jnp.zeros((tile, 1), F32)
    for at in heads_of(half):
        left = left_keys[:tile, at]
        keys = jnp.concatenate([left, own_keys[:tile, at]], axis=0)
        start = at.start // HDIM * tile
        query_grad, key_grad = head_backward(query[:, at], keys, grads[:, at], probs[start : start + tile, :])
        qg[:, at] = jnp.where(keep, query_grad, jnp.zeros_like(query_grad))
        back = key_grad[:tile].astype(BF)
        leftward[:, at] = back
        left_total += jnp.sum(back.astype(F32) * left.astype(F32), axis=-1, keepdims=True)
        own[:, at] = key_grad[tile:]
    leftsum[...] = jnp.broadcast_to(left_total, leftsum.shape)
    part = mm(qg[...], weights[...], NT)
    x_gain = acts[...].astype(F32) * vecs[:1, :]
    total = jnp.sum(x_gain * part, axis=-1, keepdims=True)
    total += jnp.sum(pick(side, x_gain, half) * own[...], axis=-1, keepdims=True)
    own[...] += pick(side, part, half)
    msg[:, :half] = pick(side, part, half, other=True).astype(BF)
    msg[:, half:] = pieces(total)


def lower_kernel(
    kept, own, msg, msg_in, left_in, sum_other, acts, vecs, dy, query, probs, left_keys, own_keys,
    dy_out, qg, key_own, leftward,
):
    tile, half = dy.shape
    side = my_side()
    keep_hi, keep_lo = is_kept(kept, True), is_kept(kept, False)
    x = acts[...].astype(F32)
    inv = inverse_rms(x)
    left = left_in[...].astype(F32)
    x_mine = pick(side, x, half)
    gain = pick(side, vecs[:1, :], half)
    gate_lo = pick(side, vecs[3:4, :], half)
    total = unpieces(msg[:, half:]) + unpieces(msg_in[:, half:])
    total += jnp.sum(x_mine * gain * left, axis=-1, keepdims=True)
    total += sum_other[:, :1] / inv
    mean_term = total / x.shape[1]
    scaled = (own[...] + left + msg_in[:, :half].astype(F32)) * gain
    change = inv * (scaled - x_mine * inv * inv * mean_term)
    dy_old = dy[...]
    dy_new = jnp.where(keep_hi, (dy_old.astype(F32) + change).astype(BF), dy_old)
    dy_out[...] = dy_new
    grads = (gate_lo * dy_new.astype(F32)).astype(BF)
    for at in heads_of(half):
        keys = jnp.concatenate([left_keys[tile:, at], own_keys[tile:, at]], axis=0)
        start = at.start // HDIM * tile
        query_grad, key_grad = head_backward(query[:, at], keys, grads[:, at], probs[start : start + tile, :])
        qg[:, at] = jnp.where(keep_lo, query_grad, jnp.zeros_like(query_grad))
        leftward[:, at] = key_grad[:tile].astype(BF)
        key_own[:, at] = key_grad[tile:]


def project_kernel(qg, weights, key_own, left_in, part_out, msg):
    half = qg.shape[1]
    side = my_side()
    part = mm(qg[...], weights[...], NT)
    mine = key_own[...] + left_in[...].astype(F32)
    first = part[:, :half] + jnp.where(side == 0, mine, 0.0)
    second = part[:, half:] + jnp.where(side == 1, mine, 0.0)
    part_out[:, :half] = first
    part_out[:, half:] = second
    msg[:, :half] = first.astype(BF)
    msg[:, half:] = second.astype(BF)


def finish_kernel(kept, part, msg_in, acts, vecs, dy_mine, dy_in, out):
    side = my_side()
    mine, other = dy_mine[...], dy_in[...]
    first = jnp.where(side == 0, mine, other)
    second = jnp.where(side == 0, other, mine)
    dy = jnp.concatenate([first, second], axis=1)
    x = acts[...].astype(F32)
    inv = inverse_rms(x)
    scaled = (part[...] + msg_in[...].astype(F32)) * vecs[2:3, :]
    mean_term = jnp.mean(x * scaled, axis=-1, keepdims=True)
    change = inv * (scaled - x * inv * inv * mean_term)
    updated = jnp.where(is_kept(kept, False), (dy.astype(F32) + change).astype(BF), dy)
    out[...] = jnp.where(side == 0, updated, dy)


def weight_grad_kernel(section_hi, flips, rows, own, other, *refs):
    grads, (kept_rows, sent_rows, scratch) = refs[:-3], refs[-3:]
    fsdp = lax.axis_index("fsdp")
    block = scratch.shape[0]
    take_own = (my_side() == 1) if section_hi else (my_side() == 0)
    parts = jnp.where(take_own, own[...], other[...])
    left = jnp.concatenate([parts[i : i + block] for i in range(0, parts.shape[0], block)], axis=1)
    right = jnp.concatenate([g[...] for g in grads], axis=0)
    scratch[...] = mm(left, right, NN).astype(BF)
    count = len(flips) // 2
    for index, flip in enumerate(flips):
        source = pl.multiple_of(jnp.bitwise_xor(fsdp, flip) * rows, rows)
        out = kept_rows if index < count else sent_rows
        target = index % count * rows
        out[target : target + rows, :] = scratch[pl.ds(source, rows), :]


def add_halves_kernel(kept_rows, arrived, mine, sent):
    total = (kept_rows[...].astype(F32) + arrived[...].astype(F32)).astype(BF)
    count = mine.shape[0]
    mine[...] = total[:count]
    sent[...] = total[count:]


def add_kernel(hi_mine, hi_arrived, lo_mine, lo_arrived, mine, theirs):
    side = my_side()
    grad_hi = (hi_mine[...].astype(F32) + hi_arrived[...].astype(F32)).astype(BF)
    grad_lo = (lo_mine[...].astype(F32) + lo_arrived[...].astype(F32)).astype(BF)
    mine[...] = jnp.where(side == 1, grad_hi, grad_lo)
    theirs[...] = jnp.where(side == 1, grad_lo, grad_hi)


def tied(value, *others):
    return lax.optimization_barrier((value, *others))[0]


def per_device(acts, grad_out, gain, gate, w_query, kept, links):
    sections = lax.axis_size("section")
    fsdps = lax.axis_size("fsdp")
    seqs = lax.axis_size("seq")
    section_idx = lax.axis_index("section")
    side = section_idx % 2
    tile, dim = acts.shape[2:]
    rows = w_query.shape[1]
    half = dim // 2
    swap_pairs = [(i, i ^ 1) for i in range(sections)]
    bits = [1 << b for b in reversed(range(seqs.bit_length() - 1))]
    top = bits[0]
    steps = [1 << b for b in reversed(range(fsdps.bit_length() - 1))]
    flips = [0]
    for step in steps:
        flips = flips + [f ^ step for f in flips]
    owners = [0]
    for step in steps:
        owners = owners + [f ^ step for f in owners]
    offsets = list(range(seqs))
    right_pairs = [(t, t + 1) for t in range(seqs - 1)]
    left_pairs = [(t + 1, t) for t in range(seqs - 1)]
    diagonal_pairs = [
        (s * seqs + t + 1, (s ^ 1) * seqs + t) for s in range(sections) for t in range(seqs - 1)
    ]
    matmul_flops = 2 * tile * dim * half
    head_flops = 2 * tile * 2 * tile * half

    def swap(value):
        return lax.ppermute(value, "section", swap_pairs)

    def across(value, offset):
        return lax.ppermute(value, "seq", [(s, s ^ offset) for s in range(seqs)])

    def along(value, flip):
        return lax.ppermute(value, "fsdp", [(f, f ^ flip) for f in range(fsdps)])

    def join(values):
        return values[0] if len(values) == 1 else jnp.concatenate(values, axis=0)

    acts_own = acts[0, 0]
    first, second = w_query[0][:, :half], w_query[0][:, half:]
    w_own, w_theirs = jnp.where(side == 0, first, second), jnp.where(side == 0, second, first)
    w_other = swap(w_theirs)
    (packed,) = call(
        pack_kernel, [sds((tile + 16, dim), BF)], 10 * tile * dim, "pack", acts_own, gain, gate
    )
    packed_in = swap(packed)

    unit = fsdps * rows
    part_shapes = [sds((seqs // 2 * unit, tile), BF)] * 2
    turned = pltpu.VMEM((dim, tile), BF)

    def to_row_owners(low, high):
        parts = [(low, [0]), (across(high, top), [0])]
        for bit in bits[1:]:
            sent = [v[b + bit * unit : b + 2 * bit * unit] for v, begins in parts for b in begins]
            arrived = across(join(sent), bit)
            parts = parts + [(arrived, [i * bit * unit for i in range(len(sent))])]
        return join([v[b : b + unit] for v, begins in parts for b in begins])

    normed_own, low_own, high_own = call(
        lambda *refs: normalize_own_kernel(offsets, rows, *refs),
        [sds((tile, dim), BF)] + part_shapes, 20 * tile * dim,
        "normalize_own", acts_own, gain, scratch=[turned],
    )
    w_hi, w_lo = call(
        select_kernel, [sds((rows, half), BF)] * 2, rows * half,
        "select_w", w_own, tied(w_other, packed, high_own),
    )
    parts_own = to_row_owners(low_own, high_own)
    def over_fsdp(shard):
        near = [shard]
        for step in steps:
            near = near + [along(join(near), step)]
        return near

    def over_seq(near, after=(), after_last=()):
        sent = [join(near[:2])] + near[2:]
        if after:
            sent = [tied(value, *after) for value in sent]
        if after_last:
            sent[-1] = tied(sent[-1], *after_last)
        return [across(value, top) for value in sent]

    def between_cores(near, far, after=(), apart=False):
        if after:
            far = [tied(value, *after) for value in far]
        places = [[(f, 0) for f in flips], [(f, top) for f in flips]]
        held = [join(near), join(far)]
        if not apart:
            held, places = [join(held)], [places[0] + places[1]]
        for bit in bits[1:]:
            held = held + [across(v, bit) for v in held]
            places = places + [[(f, o ^ bit) for f, o in place] for place in places]
        return held, places

    near_hi = over_fsdp(w_hi)
    far_hi = over_seq(near_hi, after_last=[packed_in, parts_own])
    x_hi, x_lo, normed_hi, normed_lo, keys, vecs, incoming = call(
        normalize_kernel,
        [sds((tile, dim), BF)] * 4 + [sds((2 * tile, half), BF), sds((8, dim), F32), sds((tile, half), BF)],
        30 * tile * dim,
        "normalize", acts_own, packed_in, gain, gate, grad_out[0], tied(normed_own, far_hi[0]),
    )
    left = lax.ppermute(keys, "seq", right_pairs)
    near_lo = over_fsdp(tied(w_lo, near_hi[1], packed_in))
    parts_other = swap(tied(parts_own, packed_in))
    blocks_hi, places = between_cores(near_hi, far_hi, after=[near_lo[-1], left, parts_other])
    far_lo = over_seq(near_lo, after=[left])

    def forward(name, which, normed, blocks, places):
        return call(
            lambda *refs: forward_kernel(which, places, rows, *refs),
            [sds((tile, half), BF), sds((half // HDIM * tile, 2 * tile), F32), sds((dim, half), BF)],
            matmul_flops + head_flops,
            name, normed, left, keys, *blocks, scalars=[links],
        )

    query_hi, probs_hi, weights_hi = forward("forward_hi", 0, normed_hi, blocks_hi, places)
    def over_tiles(query_grad, after=()):
        gathered = [query_grad]
        for bit in bits:
            arrived = across(join(gathered), bit)
            if after and bit == top:
                arrived = tied(arrived, *after)
            gathered = gathered + [arrived]
        return gathered

    def weight_grad(name, section_hi, gathered):
        halves = [sds((fsdps // 2 * rows, half), BF)] * 2
        return call(
            lambda *refs: weight_grad_kernel(section_hi, owners, rows, *refs),
            halves,
            2 * fsdps * rows * seqs * tile * half,
            name, parts_own, parts_other, *gathered,
            scratch=[pltpu.VMEM((fsdps * rows, half), BF)],
        )

    def over_clips(name, mine, arrived, after=()):
        if after:
            arrived = tied(arrived, *after)
        for step in reversed(steps[:-1]):
            count = mine.shape[0] // 2
            mine, sent = call(
                add_halves_kernel, [sds((count, half), BF)] * 2, 4 * count * half, name, mine, arrived
            )
            arrived = along(sent, step)
        return mine, arrived

    kept_state = None
    single = sections == 2
    for tick in range(sections // 2):
        qg_hi, own, msg, leftward, leftsum = call(
            upper_kernel,
            [
                sds((tile, half), BF),
                sds((tile, half), F32),
                sds((tile, half + HDIM), BF),
                sds((tile, half), BF),
                sds((tile, HDIM), F32),
            ],
            matmul_flops + 4 * head_flops,
            "upper", incoming, x_hi, vecs, query_hi, probs_hi, weights_hi, left, keys, scalars=[kept],
        )
        msg_in = swap(msg)
        left_in = lax.ppermute(leftward, "seq", left_pairs)
        sum_other = lax.ppermute(leftsum, ("section", "seq"), diagonal_pairs)
        exchanged = [msg_in, left_in, sum_other]
        if tick == 0:
            blocks_lo, places_lo = between_cores(near_lo, far_lo, after=exchanged, apart=True)
            query_lo, probs_lo, weights_lo = forward("forward_lo", 1, normed_lo, blocks_lo, places_lo)
        dy_mid, qg_lo, key_own, leftward_lo = call(
            lower_kernel,
            [sds((tile, half), BF), sds((tile, half), BF), sds((tile, half), F32), sds((tile, half), BF)],
            4 * head_flops,
            "lower", own, msg, msg_in, left_in, sum_other, x_hi, vecs, incoming,
            query_lo, probs_lo, left, keys, scalars=[kept],
        )
        left_in_lo = lax.ppermute(leftward_lo, "seq", left_pairs)
        dy_in = swap(dy_mid)
        if single:
            gathered_hi = over_tiles(tied(qg_hi, *exchanged), after=[qg_lo])
            mine_hi, sent_hi = weight_grad("weight_grad_hi", True, gathered_hi)
            first_hi = along(sent_hi, steps[-1])
            left_in_lo = tied(left_in_lo, mine_hi)
        part_lo, msg_lo = call(
            project_kernel, [sds((tile, dim), F32), sds((tile, dim), BF)], matmul_flops,
            "project_lo", qg_lo, weights_lo, key_own, left_in_lo,
        )
        if single:
            gathered_lo = over_tiles(qg_lo, after=[first_hi, msg_lo, dy_in])
            clips_hi = over_clips("add_pair_hi", mine_hi, first_hi)
            gathered_lo[-1] = tied(gathered_lo[-1], clips_hi[0])
            mine_lo, sent_lo = weight_grad("weight_grad_lo", False, gathered_lo)
            first_lo = along(sent_lo, steps[-1])
            clips_lo = over_clips("add_pair_lo", mine_lo, first_lo, after=clips_hi[1:])
        msg_lo_in = lax.ppermute(msg_lo, "section", [(i + 1, i) for i in range(0, sections, 2)])
        (updated,) = call(
            finish_kernel, [sds((tile, dim), BF)], 20 * tile * dim,
            "finish", part_lo, msg_lo_in, x_lo, vecs, dy_mid, dy_in, scalars=[kept],
        )
        state = (updated, qg_hi, qg_lo)
        if kept_state is None:
            kept_state = state
        else:
            active = section_idx // 2 == sections // 2 - 1 - tick
            kept_state = jax.tree.map(lambda new, old: jnp.where(active, new, old), state, kept_state)
        if tick + 1 < sections // 2:
            to_low = lax.ppermute(updated[:, :half], "section", [(i, i - 2) for i in range(2, sections, 2)])
            to_high = lax.ppermute(updated[:, half:], "section", [(i, i - 1) for i in range(2, sections, 2)])
            incoming = jnp.where(side == 0, to_low, to_high)
    result, qg_hi, qg_lo = kept_state
    if not single:
        clips = []
        for name, section_hi, query_grad in (("hi", True, qg_hi), ("lo", False, qg_lo)):
            mine, sent = weight_grad("weight_grad_" + name, section_hi, over_tiles(query_grad))
            clips.append(over_clips("add_pair_" + name, mine, along(sent, steps[-1])))
        clips_hi, clips_lo = clips

    mine, theirs = call(
        add_kernel, [sds((rows, half), BF)] * 2, 20 * rows * half,
        "add_clips", *clips_hi, clips_lo[0], tied(clips_lo[1], result),
    )
    other = swap(theirs)
    first = jnp.where(side == 0, mine, other)
    second = jnp.where(side == 0, other, mine)
    grad_rows = jnp.concatenate([first, second], axis=1)
    return (result[None, None], grad_rows[None])


def solution(mesh):
    placed = (
        P("section", "fsdp", "seq", None),
        P("fsdp", "seq", None),
        P("section", None),
        P("section", None),
        P("section", ("fsdp", "seq"), None),
        P("fsdp", None),
        P("fsdp", "seq"),
    )
    return jax.shard_map(
        per_device,
        mesh=mesh,
        in_specs=placed,
        out_specs=(P("section", "fsdp", "seq", None), P("section", ("fsdp", "seq"), None)),
        check_vma=False,
    )
```

```python
import jax
import jax.numpy as jnp
from jax import lax
from jax.experimental import pallas as pl
from jax.experimental.pallas import tpu as pltpu
from jax.sharding import PartitionSpec as P

HDIM = 128
SCALE = HDIM ** (-0.5)
EPS = 1e-06
NEG = -1e30
BF = jnp.bfloat16
F32 = jnp.float32
VLIMIT = 16 * 1024 * 1024

NN = (((1,), (0,)), ((), ()))
NT = (((1,), (1,)), ((), ()))
TN = (((0,), (0,)), ((), ()))


def mm(a, b, dims):
    return lax.dot_general(a, b, dims, preferred_element_type=F32)


def sds(shape, dtype):
    return jax.ShapeDtypeStruct(shape, dtype)


def call(kernel, outs, flops, name, *args, scalars=(), scratch=()):
    nbytes = sum(s.size * s.dtype.itemsize for s in outs) + sum(a.size * a.dtype.itemsize for a in args)
    return pl.pallas_call(
        kernel,
        out_shape=outs,
        in_specs=[pl.BlockSpec(memory_space=pltpu.SMEM)] * len(scalars)
        + [pl.BlockSpec(memory_space=pltpu.VMEM)] * len(args),
        out_specs=[pl.BlockSpec(memory_space=pltpu.VMEM)] * len(outs),
        scratch_shapes=list(scratch),
        compiler_params=pltpu.CompilerParams(vmem_limit_bytes=VLIMIT),
        cost_estimate=pl.CostEstimate(flops=flops, bytes_accessed=nbytes, transcendentals=0),
        name=name,
    )(*scalars, *args)


def my_side():
    return lax.rem(lax.axis_index("section"), 2)


def is_kept(kept, section_hi):
    hi = lax.axis_index("section") - my_side() + 1
    return kept[0, hi if section_hi else hi - 1] > 0


def pick(side, value, half, other=False):
    first = value[:, :half]
    second = value[:, half:]
    use_first = (side == 1) if other else (side == 0)
    return jnp.where(use_first, first, second)


def inverse_rms(x):
    return lax.rsqrt(jnp.mean(x * x, axis=-1, keepdims=True) + EPS)


def three_terms(value):
    high = value.astype(BF)
    rest = value - high.astype(F32)
    middle = rest.astype(BF)
    return high, middle, (rest - middle.astype(F32)).astype(BF)


def pack_kernel(acts, gain, gate, packed):
    tile = acts.shape[0]
    packed[:tile, :] = acts[...]
    shape = (packed.shape[0] - tile, acts.shape[1])
    row = lax.broadcasted_iota(jnp.int32, shape, 0)
    terms = jnp.zeros(shape, F32)
    for index, term in enumerate(three_terms(gain[...]) + three_terms(gate[...])):
        terms = jnp.where(row == index, jnp.broadcast_to(term.astype(F32), shape), terms)
    packed[tile:, :] = terms.astype(BF)


def select_kernel(own, other, hi, lo):
    side = my_side()
    hi[...] = jnp.where(side == 1, own[...], other[...])
    lo[...] = jnp.where(side == 1, other[...], own[...])


def row_blocks(value, offsets, rows, parts, turned):
    seqs = len(offsets)
    block = parts[0].shape[0] // (seqs // 2)
    seq = lax.axis_index("seq")
    turned[...] = value.astype(F32).T.astype(BF)
    for offset in offsets:
        part = parts[0] if offset < seqs // 2 else parts[1]
        base = offset % (seqs // 2) * block
        for f in range(block // rows):
            source = pl.multiple_of((f * seqs + jnp.bitwise_xor(seq, offset)) * rows, rows)
            part[base + f * rows : base + (f + 1) * rows, :] = turned[pl.ds(source, rows), :]


def normalize_own_kernel(offsets, rows, acts, gain, normed, low, high, turned):
    x = acts[...].astype(F32)
    value = (x * inverse_rms(x) * gain[...]).astype(BF)
    normed[...] = value
    row_blocks(value, offsets, rows, (low, high), turned)


def normalize_kernel(acts, packed, gain, gate, dy_full, normed_own, *outs):
    xs, normed, (keys, vecs, dy) = outs[:2], outs[2:4], outs[4:]
    tile, half = dy.shape
    extra = packed[tile:, :].astype(F32)
    gain_in = extra[0:1] + extra[1:2] + extra[2:3]
    gate_in = extra[3:4] + extra[4:5] + extra[5:6]
    x = packed[:tile, :].astype(F32)
    value = (x * inverse_rms(x) * gain_in).astype(BF)
    own = acts[...], normed_own[...], gain[...], gate[...]
    other = packed[:tile, :], value, gain_in, gate_in
    side = my_side()
    for which in range(2):
        take_own = side == 1 - which
        x_low, rounded, gain_row, gate_row = [jnp.where(take_own, a, b) for a, b in zip(own, other)]
        xs[which][...] = x_low
        normed[which][...] = rounded
        vecs[2 * which : 2 * which + 1, :] = gain_row
        vecs[2 * which + 1 : 2 * which + 2, :] = gate_row
        keys[which * tile : (which + 1) * tile, :] = pick(side, rounded, half)
    dy[...] = pick(side, dy_full[...], half)


def head_probs(query, keys, linked):
    scores = mm(query, keys, NT) * SCALE
    column = lax.broadcasted_iota(jnp.int32, scores.shape, 1)
    scores = jnp.where(jnp.logical_or(column >= scores.shape[1] // 2, linked), scores, NEG)
    exps = jnp.exp(scores - jnp.max(scores, axis=-1, keepdims=True))
    return exps / jnp.sum(exps, axis=-1, keepdims=True)


def head_backward(query, keys, grads, probs):
    prob_grad = mm(grads, keys, NT)
    row_delta = jnp.sum(probs * prob_grad, axis=-1, keepdims=True)
    score_grad = (probs * (prob_grad - row_delta) * SCALE).astype(BF)
    query_grad = mm(score_grad, keys, NN).astype(BF)
    key_grad = mm(
        jnp.concatenate([score_grad, probs.astype(BF)], axis=0),
        jnp.concatenate([query, grads], axis=0),
        TN,
    )
    return query_grad, key_grad


def pieces(column):
    rows = column.shape[0]
    lane = lax.broadcasted_iota(jnp.int32, (rows, HDIM), 1)
    high, middle, low = [jnp.broadcast_to(p.astype(F32), (rows, HDIM)) for p in three_terms(column)]
    value = jnp.where(lane == 0, high, jnp.where(lane == 1, middle, jnp.where(lane == 2, low, 0.0)))
    return value.astype(BF)


def unpieces(block):
    return jnp.sum(block.astype(F32), axis=-1, keepdims=True)


def heads_of(half):
    return [slice(h * HDIM, (h + 1) * HDIM) for h in range(half // HDIM)]


def pairs_of(half):
    step = 2 * HDIM if half % (2 * HDIM) == 0 else HDIM
    return [slice(c, c + step) for c in range(0, half, step)]


def forward_kernel(which, places, rows, links, normed, left_keys, own_keys, *rest):
    blocks = rest[: len(places)]
    query_out, probs_out, weights = rest[len(places) :]
    tile, half = query_out.shape
    token = slice(which * tile, (which + 1) * tile)
    seqs = lax.axis_size("seq")
    fsdp, seq = lax.axis_index("fsdp"), lax.axis_index("seq")
    linked = jnp.logical_and(links[0, 0] > 0, seq > 0)
    for block, place in zip(blocks, places):
        for index, (flip, offset) in enumerate(place):
            f = jnp.bitwise_xor(fsdp, flip)
            target = pl.multiple_of((f * seqs + jnp.bitwise_xor(seq, offset)) * rows, rows)
            weights[pl.ds(target, rows), :] = block[index * rows : (index + 1) * rows, :]
    tokens = normed[...]
    for cols in pairs_of(half):
        query = mm(tokens, weights[:, cols], NN).astype(BF)
        query_out[:, cols] = query
        for sub in heads_of(cols.stop - cols.start):
            at = slice(cols.start + sub.start, cols.start + sub.stop)
            keys = jnp.concatenate([left_keys[token, at], own_keys[token, at]], axis=0)
            start = at.start // HDIM * tile
            probs_out[start : start + tile, :] = head_probs(query[:, sub], keys, linked)


def upper_kernel(
    kept, dy, acts, vecs, query, probs, weights, left_keys, own_keys, qg, own, msg, leftward, leftsum
):
    tile, half = dy.shape
    side = my_side()
    keep = is_kept(kept, True)
    gate = pick(side, vecs[1:2, :], half)
    grads = (gate * dy[...].astype(F32)).astype(BF)
    left_total = jnp.zeros((tile, 1), F32)
    for at in heads_of(half):
        left = left_keys[:tile, at]
        keys = jnp.concatenate([left, own_keys[:tile, at]], axis=0)
        start = at.start // HDIM * tile
        query_grad, key_grad = head_backward(query[:, at], keys, grads[:, at], probs[start : start + tile, :])
        qg[:, at] = jnp.where(keep, query_grad, jnp.zeros_like(query_grad))
        back = key_grad[:tile].astype(BF)
        leftward[:, at] = back
        left_total += jnp.sum(back.astype(F32) * left.astype(F32), axis=-1, keepdims=True)
        own[:, at] = key_grad[tile:]
    leftsum[...] = jnp.broadcast_to(left_total, leftsum.shape)
    part = mm(qg[...], weights[...], NT)
    x_gain = acts[...].astype(F32) * vecs[:1, :]
    total = jnp.sum(x_gain * part, axis=-1, keepdims=True)
    total += jnp.sum(pick(side, x_gain, half) * own[...], axis=-1, keepdims=True)
    own[...] += pick(side, part, half)
    msg[:, :half] = pick(side, part, half, other=True).astype(BF)
    msg[:, half:] = pieces(total)


def lower_kernel(
    kept, own, msg, msg_in, left_in, sum_other, acts, vecs, dy, query, probs, left_keys, own_keys,
    dy_out, qg, key_own, leftward,
):
    tile, half = dy.shape
    side = my_side()
    keep_hi, keep_lo = is_kept(kept, True), is_kept(kept, False)
    x = acts[...].astype(F32)
    inv = inverse_rms(x)
    left = left_in[...].astype(F32)
    x_mine = pick(side, x, half)
    gain = pick(side, vecs[:1, :], half)
    gate_lo = pick(side, vecs[3:4, :], half)
    total = unpieces(msg[:, half:]) + unpieces(msg_in[:, half:])
    total += jnp.sum(x_mine * gain * left, axis=-1, keepdims=True)
    total += sum_other[:, :1] / inv
    mean_term = total / x.shape[1]
    scaled = (own[...] + left + msg_in[:, :half].astype(F32)) * gain
    change = inv * (scaled - x_mine * inv * inv * mean_term)
    dy_old = dy[...]
    dy_new = jnp.where(keep_hi, (dy_old.astype(F32) + change).astype(BF), dy_old)
    dy_out[...] = dy_new
    grads = (gate_lo * dy_new.astype(F32)).astype(BF)
    for at in heads_of(half):
        keys = jnp.concatenate([left_keys[tile:, at], own_keys[tile:, at]], axis=0)
        start = at.start // HDIM * tile
        query_grad, key_grad = head_backward(query[:, at], keys, grads[:, at], probs[start : start + tile, :])
        qg[:, at] = jnp.where(keep_lo, query_grad, jnp.zeros_like(query_grad))
        leftward[:, at] = key_grad[:tile].astype(BF)
        key_own[:, at] = key_grad[tile:]


def project_kernel(qg, weights, key_own, left_in, part_out, msg):
    half = qg.shape[1]
    side = my_side()
    part = mm(qg[...], weights[...], NT)
    mine = key_own[...] + left_in[...].astype(F32)
    first = part[:, :half] + jnp.where(side == 0, mine, 0.0)
    second = part[:, half:] + jnp.where(side == 1, mine, 0.0)
    part_out[:, :half] = first
    part_out[:, half:] = second
    msg[:, :half] = first.astype(BF)
    msg[:, half:] = second.astype(BF)


def finish_kernel(kept, part, msg_in, acts, vecs, dy_mine, dy_in, out):
    side = my_side()
    mine, other = dy_mine[...], dy_in[...]
    first = jnp.where(side == 0, mine, other)
    second = jnp.where(side == 0, other, mine)
    dy = jnp.concatenate([first, second], axis=1)
    x = acts[...].astype(F32)
    inv = inverse_rms(x)
    scaled = (part[...] + msg_in[...].astype(F32)) * vecs[2:3, :]
    mean_term = jnp.mean(x * scaled, axis=-1, keepdims=True)
    change = inv * (scaled - x * inv * inv * mean_term)
    updated = jnp.where(is_kept(kept, False), (dy.astype(F32) + change).astype(BF), dy)
    out[...] = jnp.where(side == 0, updated, dy)


def weight_grad_kernel(section_hi, flips, rows, own, other, *refs):
    grads, (kept_rows, sent_rows, scratch) = refs[:-3], refs[-3:]
    fsdp = lax.axis_index("fsdp")
    block = scratch.shape[0]
    take_own = (my_side() == 1) if section_hi else (my_side() == 0)
    parts = jnp.where(take_own, own[...], other[...])
    left = jnp.concatenate([parts[i : i + block] for i in range(0, parts.shape[0], block)], axis=1)
    right = jnp.concatenate([g[...] for g in grads], axis=0)
    scratch[...] = mm(left, right, NN).astype(BF)
    count = len(flips) // 2
    for index, flip in enumerate(flips):
        source = pl.multiple_of(jnp.bitwise_xor(fsdp, flip) * rows, rows)
        out = kept_rows if index < count else sent_rows
        target = index % count * rows
        out[target : target + rows, :] = scratch[pl.ds(source, rows), :]


def add_halves_kernel(kept_rows, arrived, mine, sent):
    total = (kept_rows[...].astype(F32) + arrived[...].astype(F32)).astype(BF)
    count = mine.shape[0]
    mine[...] = total[:count]
    sent[...] = total[count:]


def add_kernel(hi_mine, hi_arrived, lo_mine, lo_arrived, mine, theirs):
    side = my_side()
    grad_hi = (hi_mine[...].astype(F32) + hi_arrived[...].astype(F32)).astype(BF)
    grad_lo = (lo_mine[...].astype(F32) + lo_arrived[...].astype(F32)).astype(BF)
    mine[...] = jnp.where(side == 1, grad_hi, grad_lo)
    theirs[...] = jnp.where(side == 1, grad_lo, grad_hi)


def tied(value, *others):
    return lax.optimization_barrier((value, *others))[0]


def per_device(acts, grad_out, gain, gate, w_query, kept, links):
    sections = lax.axis_size("section")
    fsdps = lax.axis_size("fsdp")
    seqs = lax.axis_size("seq")
    section_idx = lax.axis_index("section")
    side = section_idx % 2
    tile, dim = acts.shape[2:]
    rows = w_query.shape[1]
    half = dim // 2
    swap_pairs = [(i, i ^ 1) for i in range(sections)]
    bits = [1 << b for b in reversed(range(seqs.bit_length() - 1))]
    top = bits[0]
    steps = [1 << b for b in reversed(range(fsdps.bit_length() - 1))]
    flips = [0]
    for step in steps:
        flips = flips + [f ^ step for f in flips]
    owners = [0]
    for step in steps:
        owners = owners + [f ^ step for f in owners]
    offsets = list(range(seqs))
    right_pairs = [(t, t + 1) for t in range(seqs - 1)]
    left_pairs = [(t + 1, t) for t in range(seqs - 1)]
    diagonal_pairs = [
        (s * seqs + t + 1, (s ^ 1) * seqs + t) for s in range(sections) for t in range(seqs - 1)
    ]
    matmul_flops = 2 * tile * dim * half
    head_flops = 2 * tile * 2 * tile * half

    def swap(value):
        return lax.ppermute(value, "section", swap_pairs)

    def across(value, offset):
        return lax.ppermute(value, "seq", [(s, s ^ offset) for s in range(seqs)])

    def along(value, flip):
        return lax.ppermute(value, "fsdp", [(f, f ^ flip) for f in range(fsdps)])

    def join(values):
        return values[0] if len(values) == 1 else jnp.concatenate(values, axis=0)

    acts_own = acts[0, 0]
    first, second = w_query[0][:, :half], w_query[0][:, half:]
    w_own, w_theirs = jnp.where(side == 0, first, second), jnp.where(side == 0, second, first)
    w_other = swap(w_theirs)
    (packed,) = call(
        pack_kernel, [sds((tile + 16, dim), BF)], 10 * tile * dim, "pack", acts_own, gain, gate
    )
    packed_in = swap(packed)

    unit = fsdps * rows
    part_shapes = [sds((seqs // 2 * unit, tile), BF)] * 2
    turned = pltpu.VMEM((dim, tile), BF)

    def to_row_owners(low, high):
        parts = [(low, [0]), (across(high, top), [0])]
        for bit in bits[1:]:
            sent = [v[b + bit * unit : b + 2 * bit * unit] for v, begins in parts for b in begins]
            arrived = across(join(sent), bit)
            parts = parts + [(arrived, [i * bit * unit for i in range(len(sent))])]
        return join([v[b : b + unit] for v, begins in parts for b in begins])

    normed_own, low_own, high_own = call(
        lambda *refs: normalize_own_kernel(offsets, rows, *refs),
        [sds((tile, dim), BF)] + part_shapes, 20 * tile * dim,
        "normalize_own", acts_own, gain, scratch=[turned],
    )
    w_hi, w_lo = call(
        select_kernel, [sds((rows, half), BF)] * 2, rows * half,
        "select_w", w_own, tied(w_other, packed, high_own),
    )
    parts_own = to_row_owners(low_own, high_own)
    def over_fsdp(shard):
        near = [shard]
        for step in steps:
            near = near + [along(join(near), step)]
        return near

    def over_seq(near, after=(), after_last=()):
        sent = [join(near[:2])] + near[2:]
        if after:
            sent = [tied(value, *after) for value in sent]
        if after_last:
            sent[-1] = tied(sent[-1], *after_last)
        return [across(value, top) for value in sent]

    def between_cores(near, far, after=(), apart=False):
        if after:
            far = [tied(value, *after) for value in far]
        places = [[(f, 0) for f in flips], [(f, top) for f in flips]]
        held = [join(near), join(far)]
        if not apart:
            held, places = [join(held)], [places[0] + places[1]]
        for bit in bits[1:]:
            held = held + [across(v, bit) for v in held]
            places = places + [[(f, o ^ bit) for f, o in place] for place in places]
        return held, places

    near_hi = over_fsdp(w_hi)
    far_hi = over_seq(near_hi, after_last=[packed_in, parts_own])
    x_hi, x_lo, normed_hi, normed_lo, keys, vecs, incoming = call(
        normalize_kernel,
        [sds((tile, dim), BF)] * 4 + [sds((2 * tile, half), BF), sds((8, dim), F32), sds((tile, half), BF)],
        30 * tile * dim,
        "normalize", acts_own, packed_in, gain, gate, grad_out[0], tied(normed_own, far_hi[0]),
    )
    left = lax.ppermute(keys, "seq", right_pairs)
    near_lo = over_fsdp(tied(w_lo, near_hi[1], packed_in))
    parts_other = swap(tied(parts_own, packed_in))
    blocks_hi, places = between_cores(near_hi, far_hi, after=[near_lo[-1], left, parts_other])
    far_lo = over_seq(near_lo, after=[left])

    def forward(name, which, normed, blocks, places):
        return call(
            lambda *refs: forward_kernel(which, places, rows, *refs),
            [sds((tile, half), BF), sds((half // HDIM * tile, 2 * tile), F32), sds((dim, half), BF)],
            matmul_flops + head_flops,
            name, normed, left, keys, *blocks, scalars=[links],
        )

    query_hi, probs_hi, weights_hi = forward("forward_hi", 0, normed_hi, blocks_hi, places)
    def over_tiles(query_grad, after=()):
        gathered = [query_grad]
        for bit in bits:
            arrived = across(join(gathered), bit)
            if after and bit == top:
                arrived = tied(arrived, *after)
            gathered = gathered + [arrived]
        return gathered

    def weight_grad(name, section_hi, gathered):
        halves = [sds((fsdps // 2 * rows, half), BF)] * 2
        return call(
            lambda *refs: weight_grad_kernel(section_hi, owners, rows, *refs),
            halves,
            2 * fsdps * rows * seqs * tile * half,
            name, parts_own, parts_other, *gathered,
            scratch=[pltpu.VMEM((fsdps * rows, half), BF)],
        )

    def over_clips(name, mine, arrived, after=()):
        if after:
            arrived = tied(arrived, *after)
        for step in reversed(steps[:-1]):
            count = mine.shape[0] // 2
            mine, sent = call(
                add_halves_kernel, [sds((count, half), BF)] * 2, 4 * count * half, name, mine, arrived
            )
            arrived = along(sent, step)
        return mine, arrived

    kept_state = None
    single = sections == 2
    for tick in range(sections // 2):
        qg_hi, own, msg, leftward, leftsum = call(
            upper_kernel,
            [
                sds((tile, half), BF),
                sds((tile, half), F32),
                sds((tile, half + HDIM), BF),
                sds((tile, half), BF),
                sds((tile, HDIM), F32),
            ],
            matmul_flops + 4 * head_flops,
            "upper", incoming, x_hi, vecs, query_hi, probs_hi, weights_hi, left, keys, scalars=[kept],
        )
        msg_in = swap(msg)
        left_in = lax.ppermute(leftward, "seq", left_pairs)
        sum_other = lax.ppermute(leftsum, ("section", "seq"), diagonal_pairs)
        exchanged = [msg_in, left_in, sum_other]
        if tick == 0:
            blocks_lo, places_lo = between_cores(near_lo, far_lo, after=exchanged, apart=True)
            query_lo, probs_lo, weights_lo = forward("forward_lo", 1, normed_lo, blocks_lo, places_lo)
        dy_mid, qg_lo, key_own, leftward_lo = call(
            lower_kernel,
            [sds((tile, half), BF), sds((tile, half), BF), sds((tile, half), F32), sds((tile, half), BF)],
            4 * head_flops,
            "lower", own, msg, msg_in, left_in, sum_other, x_hi, vecs, incoming,
            query_lo, probs_lo, left, keys, scalars=[kept],
        )
        left_in_lo = lax.ppermute(leftward_lo, "seq", left_pairs)
        dy_in = swap(dy_mid)
        if single:
            gathered_hi = over_tiles(tied(qg_hi, *exchanged), after=[qg_lo])
            mine_hi, sent_hi = weight_grad("weight_grad_hi", True, gathered_hi)
            first_hi = along(sent_hi, steps[-1])
            clips_hi = over_clips("add_pair_hi", mine_hi, first_hi)
            left_in_lo = tied(left_in_lo, clips_hi[1], dy_in)
        part_lo, msg_lo = call(
            project_kernel, [sds((tile, dim), F32), sds((tile, dim), BF)], matmul_flops,
            "project_lo", qg_lo, weights_lo, key_own, left_in_lo,
        )
        if single:
            gathered_lo = over_tiles(qg_lo, after=[first_hi])
            gathered_lo[-1] = tied(gathered_lo[-1], clips_hi[0])
            mine_lo, sent_lo = weight_grad("weight_grad_lo", False, gathered_lo)
            first_lo = along(sent_lo, steps[-1])
            clips_lo = over_clips("add_pair_lo", mine_lo, first_lo, after=clips_hi[1:])
        msg_lo_in = lax.ppermute(msg_lo, "section", [(i + 1, i) for i in range(0, sections, 2)])
        (updated,) = call(
            finish_kernel, [sds((tile, dim), BF)], 20 * tile * dim,
            "finish", part_lo, msg_lo_in, x_lo, vecs, dy_mid, dy_in, scalars=[kept],
        )
        state = (updated, qg_hi, qg_lo)
        if kept_state is None:
            kept_state = state
        else:
            active = section_idx // 2 == sections // 2 - 1 - tick
            kept_state = jax.tree.map(lambda new, old: jnp.where(active, new, old), state, kept_state)
        if tick + 1 < sections // 2:
            to_low = lax.ppermute(updated[:, :half], "section", [(i, i - 2) for i in range(2, sections, 2)])
            to_high = lax.ppermute(updated[:, half:], "section", [(i, i - 1) for i in range(2, sections, 2)])
            incoming = jnp.where(side == 0, to_low, to_high)
    result, qg_hi, qg_lo = kept_state
    if not single:
        clips = []
        for name, section_hi, query_grad in (("hi", True, qg_hi), ("lo", False, qg_lo)):
            mine, sent = weight_grad("weight_grad_" + name, section_hi, over_tiles(query_grad))
            clips.append(over_clips("add_pair_" + name, mine, along(sent, steps[-1])))
        clips_hi, clips_lo = clips

    mine, theirs = call(
        add_kernel, [sds((rows, half), BF)] * 2, 20 * rows * half,
        "add_clips", *clips_hi, *clips_lo,
    )
    other = swap(theirs)
    first = jnp.where(side == 0, mine, other)
    second = jnp.where(side == 0, other, mine)
    grad_rows = jnp.concatenate([first, second], axis=1)
    return (result[None, None], grad_rows[None])


def solution(mesh):
    placed = (
        P("section", "fsdp", "seq", None),
        P("fsdp", "seq", None),
        P("section", None),
        P("section", None),
        P("section", ("fsdp", "seq"), None),
        P("fsdp", None),
        P("fsdp", "seq"),
    )
    return jax.shard_map(
        per_device,
        mesh=mesh,
        in_specs=placed,
        out_specs=(P("section", "fsdp", "seq", None), P("section", ("fsdp", "seq"), None)),
        check_vma=False,
    )
```

```python
import jax
import jax.numpy as jnp
from jax import lax
from jax.experimental import pallas as pl
from jax.experimental.pallas import tpu as pltpu
from jax.sharding import PartitionSpec as P

HDIM = 128
SCALE = HDIM ** (-0.5)
EPS = 1e-06
NEG = -1e30
BF = jnp.bfloat16
F32 = jnp.float32
VLIMIT = 16 * 1024 * 1024

NN = (((1,), (0,)), ((), ()))
NT = (((1,), (1,)), ((), ()))
TN = (((0,), (0,)), ((), ()))


def mm(a, b, dims):
    return lax.dot_general(a, b, dims, preferred_element_type=F32)


def sds(shape, dtype):
    return jax.ShapeDtypeStruct(shape, dtype)


def call(kernel, outs, flops, name, *args, scalars=(), scratch=()):
    nbytes = sum(s.size * s.dtype.itemsize for s in outs) + sum(a.size * a.dtype.itemsize for a in args)
    return pl.pallas_call(
        kernel,
        out_shape=outs,
        in_specs=[pl.BlockSpec(memory_space=pltpu.SMEM)] * len(scalars)
        + [pl.BlockSpec(memory_space=pltpu.VMEM)] * len(args),
        out_specs=[pl.BlockSpec(memory_space=pltpu.VMEM)] * len(outs),
        scratch_shapes=list(scratch),
        compiler_params=pltpu.CompilerParams(vmem_limit_bytes=VLIMIT),
        cost_estimate=pl.CostEstimate(flops=flops, bytes_accessed=nbytes, transcendentals=0),
        name=name,
    )(*scalars, *args)


def my_side():
    return lax.rem(lax.axis_index("section"), 2)


def is_kept(kept, section_hi):
    hi = lax.axis_index("section") - my_side() + 1
    return kept[0, hi if section_hi else hi - 1] > 0


def pick(side, value, half, other=False):
    first = value[:, :half]
    second = value[:, half:]
    use_first = (side == 1) if other else (side == 0)
    return jnp.where(use_first, first, second)


def inverse_rms(x):
    return lax.rsqrt(jnp.mean(x * x, axis=-1, keepdims=True) + EPS)


def three_terms(value):
    high = value.astype(BF)
    rest = value - high.astype(F32)
    middle = rest.astype(BF)
    return high, middle, (rest - middle.astype(F32)).astype(BF)


def pack_kernel(acts, gain, gate, packed):
    tile = acts.shape[0]
    packed[:tile, :] = acts[...]
    shape = (packed.shape[0] - tile, acts.shape[1])
    row = lax.broadcasted_iota(jnp.int32, shape, 0)
    terms = jnp.zeros(shape, F32)
    for index, term in enumerate(three_terms(gain[...]) + three_terms(gate[...])):
        terms = jnp.where(row == index, jnp.broadcast_to(term.astype(F32), shape), terms)
    packed[tile:, :] = terms.astype(BF)


def select_kernel(own, other, hi, lo):
    side = my_side()
    hi[...] = jnp.where(side == 1, own[...], other[...])
    lo[...] = jnp.where(side == 1, other[...], own[...])


def row_blocks(value, offsets, rows, parts, turned):
    seqs = len(offsets)
    block = parts[0].shape[0] // (seqs // 2)
    seq = lax.axis_index("seq")
    turned[...] = value.astype(F32).T.astype(BF)
    for offset in offsets:
        part = parts[0] if offset < seqs // 2 else parts[1]
        base = offset % (seqs // 2) * block
        for f in range(block // rows):
            source = pl.multiple_of((f * seqs + jnp.bitwise_xor(seq, offset)) * rows, rows)
            part[base + f * rows : base + (f + 1) * rows, :] = turned[pl.ds(source, rows), :]


def normalize_own_kernel(offsets, rows, acts, gain, normed, low, high, turned):
    x = acts[...].astype(F32)
    value = (x * inverse_rms(x) * gain[...]).astype(BF)
    normed[...] = value
    row_blocks(value, offsets, rows, (low, high), turned)


def normalize_kernel(acts, packed, gain, gate, dy_full, normed_own, *outs):
    xs, normed, (keys, vecs, dy) = outs[:2], outs[2:4], outs[4:]
    tile, half = dy.shape
    extra = packed[tile:, :].astype(F32)
    gain_in = extra[0:1] + extra[1:2] + extra[2:3]
    gate_in = extra[3:4] + extra[4:5] + extra[5:6]
    x = packed[:tile, :].astype(F32)
    value = (x * inverse_rms(x) * gain_in).astype(BF)
    own = acts[...], normed_own[...], gain[...], gate[...]
    other = packed[:tile, :], value, gain_in, gate_in
    side = my_side()
    for which in range(2):
        take_own = side == 1 - which
        x_low, rounded, gain_row, gate_row = [jnp.where(take_own, a, b) for a, b in zip(own, other)]
        xs[which][...] = x_low
        normed[which][...] = rounded
        vecs[2 * which : 2 * which + 1, :] = gain_row
        vecs[2 * which + 1 : 2 * which + 2, :] = gate_row
        keys[which * tile : (which + 1) * tile, :] = pick(side, rounded, half)
    dy[...] = pick(side, dy_full[...], half)


def head_probs(query, keys, linked):
    scores = mm(query, keys, NT) * SCALE
    column = lax.broadcasted_iota(jnp.int32, scores.shape, 1)
    scores = jnp.where(jnp.logical_or(column >= scores.shape[1] // 2, linked), scores, NEG)
    exps = jnp.exp(scores - jnp.max(scores, axis=-1, keepdims=True))
    return exps / jnp.sum(exps, axis=-1, keepdims=True)


def head_backward(query, keys, grads, probs):
    prob_grad = mm(grads, keys, NT)
    row_delta = jnp.sum(probs * prob_grad, axis=-1, keepdims=True)
    score_grad = (probs * (prob_grad - row_delta) * SCALE).astype(BF)
    query_grad = mm(score_grad, keys, NN).astype(BF)
    key_grad = mm(
        jnp.concatenate([score_grad, probs.astype(BF)], axis=0),
        jnp.concatenate([query, grads], axis=0),
        TN,
    )
    return query_grad, key_grad


def pieces(column):
    rows = column.shape[0]
    lane = lax.broadcasted_iota(jnp.int32, (rows, HDIM), 1)
    high, middle, low = [jnp.broadcast_to(p.astype(F32), (rows, HDIM)) for p in three_terms(column)]
    value = jnp.where(lane == 0, high, jnp.where(lane == 1, middle, jnp.where(lane == 2, low, 0.0)))
    return value.astype(BF)


def unpieces(block):
    return jnp.sum(block.astype(F32), axis=-1, keepdims=True)


def heads_of(half):
    return [slice(h * HDIM, (h + 1) * HDIM) for h in range(half // HDIM)]


def pairs_of(half):
    step = 2 * HDIM if half % (2 * HDIM) == 0 else HDIM
    return [slice(c, c + step) for c in range(0, half, step)]


def forward_kernel(which, places, rows, links, normed, left_keys, own_keys, *rest):
    blocks = rest[: len(places)]
    query_out, probs_out, weights = rest[len(places) :]
    tile, half = query_out.shape
    token = slice(which * tile, (which + 1) * tile)
    seqs = lax.axis_size("seq")
    fsdp, seq = lax.axis_index("fsdp"), lax.axis_index("seq")
    linked = jnp.logical_and(links[0, 0] > 0, seq > 0)
    for block, place in zip(blocks, places):
        for index, (flip, offset) in enumerate(place):
            f = jnp.bitwise_xor(fsdp, flip)
            target = pl.multiple_of((f * seqs + jnp.bitwise_xor(seq, offset)) * rows, rows)
            weights[pl.ds(target, rows), :] = block[index * rows : (index + 1) * rows, :]
    tokens = normed[...]
    for cols in pairs_of(half):
        query = mm(tokens, weights[:, cols], NN).astype(BF)
        query_out[:, cols] = query
        for sub in heads_of(cols.stop - cols.start):
            at = slice(cols.start + sub.start, cols.start + sub.stop)
            keys = jnp.concatenate([left_keys[token, at], own_keys[token, at]], axis=0)
            start = at.start // HDIM * tile
            probs_out[start : start + tile, :] = head_probs(query[:, sub], keys, linked)


def upper_kernel(
    kept, dy, acts, vecs, query, probs, weights, left_keys, own_keys, qg, own, msg, leftward, leftsum
):
    tile, half = dy.shape
    side = my_side()
    keep = is_kept(kept, True)
    gate = pick(side, vecs[1:2, :], half)
    grads = (gate * dy[...].astype(F32)).astype(BF)
    left_total = jnp.zeros((tile, 1), F32)
    for at in heads_of(half):
        left = left_keys[:tile, at]
        keys = jnp.concatenate([left, own_keys[:tile, at]], axis=0)
        start = at.start // HDIM * tile
        query_grad, key_grad = head_backward(query[:, at], keys, grads[:, at], probs[start : start + tile, :])
        qg[:, at] = jnp.where(keep, query_grad, jnp.zeros_like(query_grad))
        back = key_grad[:tile].astype(BF)
        leftward[:, at] = back
        left_total += jnp.sum(back.astype(F32) * left.astype(F32), axis=-1, keepdims=True)
        own[:, at] = key_grad[tile:]
    leftsum[...] = jnp.broadcast_to(left_total, leftsum.shape)
    part = mm(qg[...], weights[...], NT)
    x_gain = acts[...].astype(F32) * vecs[:1, :]
    total = jnp.sum(x_gain * part, axis=-1, keepdims=True)
    total += jnp.sum(pick(side, x_gain, half) * own[...], axis=-1, keepdims=True)
    own[...] += pick(side, part, half)
    msg[:, :half] = pick(side, part, half, other=True).astype(BF)
    msg[:, half:] = pieces(total)


def lower_kernel(
    kept, own, msg, msg_in, left_in, sum_other, acts, vecs, dy, query, probs, left_keys, own_keys,
    dy_out, qg, key_own, leftward,
):
    tile, half = dy.shape
    side = my_side()
    keep_hi, keep_lo = is_kept(kept, True), is_kept(kept, False)
    x = acts[...].astype(F32)
    inv = inverse_rms(x)
    left = left_in[...].astype(F32)
    x_mine = pick(side, x, half)
    gain = pick(side, vecs[:1, :], half)
    gate_lo = pick(side, vecs[3:4, :], half)
    total = unpieces(msg[:, half:]) + unpieces(msg_in[:, half:])
    total += jnp.sum(x_mine * gain * left, axis=-1, keepdims=True)
    total += sum_other[:, :1] / inv
    mean_term = total / x.shape[1]
    scaled = (own[...] + left + msg_in[:, :half].astype(F32)) * gain
    change = inv * (scaled - x_mine * inv * inv * mean_term)
    dy_old = dy[...]
    dy_new = jnp.where(keep_hi, (dy_old.astype(F32) + change).astype(BF), dy_old)
    dy_out[...] = dy_new
    grads = (gate_lo * dy_new.astype(F32)).astype(BF)
    for at in heads_of(half):
        keys = jnp.concatenate([left_keys[tile:, at], own_keys[tile:, at]], axis=0)
        start = at.start // HDIM * tile
        query_grad, key_grad = head_backward(query[:, at], keys, grads[:, at], probs[start : start + tile, :])
        qg[:, at] = jnp.where(keep_lo, query_grad, jnp.zeros_like(query_grad))
        leftward[:, at] = key_grad[:tile].astype(BF)
        key_own[:, at] = key_grad[tile:]


def project_kernel(qg, weights, key_own, left_in, part_out, msg):
    half = qg.shape[1]
    side = my_side()
    part = mm(qg[...], weights[...], NT)
    mine = key_own[...] + left_in[...].astype(F32)
    first = part[:, :half] + jnp.where(side == 0, mine, 0.0)
    second = part[:, half:] + jnp.where(side == 1, mine, 0.0)
    part_out[:, :half] = first
    part_out[:, half:] = second
    msg[:, :half] = first.astype(BF)
    msg[:, half:] = second.astype(BF)


def finish_kernel(kept, part, msg_in, acts, vecs, dy_mine, dy_in, out):
    side = my_side()
    mine, other = dy_mine[...], dy_in[...]
    first = jnp.where(side == 0, mine, other)
    second = jnp.where(side == 0, other, mine)
    dy = jnp.concatenate([first, second], axis=1)
    x = acts[...].astype(F32)
    inv = inverse_rms(x)
    scaled = (part[...] + msg_in[...].astype(F32)) * vecs[2:3, :]
    mean_term = jnp.mean(x * scaled, axis=-1, keepdims=True)
    change = inv * (scaled - x * inv * inv * mean_term)
    updated = jnp.where(is_kept(kept, False), (dy.astype(F32) + change).astype(BF), dy)
    out[...] = jnp.where(side == 0, updated, dy)


def weight_grad_kernel(section_hi, flips, rows, own, other, *refs):
    grads, (kept_rows, sent_rows, scratch) = refs[:-3], refs[-3:]
    fsdp = lax.axis_index("fsdp")
    block = scratch.shape[0]
    take_own = (my_side() == 1) if section_hi else (my_side() == 0)
    parts = jnp.where(take_own, own[...], other[...])
    left = jnp.concatenate([parts[i : i + block] for i in range(0, parts.shape[0], block)], axis=1)
    right = jnp.concatenate([g[...] for g in grads], axis=0)
    scratch[...] = mm(left, right, NN).astype(BF)
    count = len(flips) // 2
    for index, flip in enumerate(flips):
        source = pl.multiple_of(jnp.bitwise_xor(fsdp, flip) * rows, rows)
        out = kept_rows if index < count else sent_rows
        target = index % count * rows
        out[target : target + rows, :] = scratch[pl.ds(source, rows), :]


def add_halves_kernel(kept_rows, arrived, mine, sent):
    total = (kept_rows[...].astype(F32) + arrived[...].astype(F32)).astype(BF)
    count = mine.shape[0]
    mine[...] = total[:count]
    sent[...] = total[count:]


def add_kernel(hi_mine, hi_arrived, lo_mine, lo_arrived, mine, theirs):
    side = my_side()
    grad_hi = (hi_mine[...].astype(F32) + hi_arrived[...].astype(F32)).astype(BF)
    grad_lo = (lo_mine[...].astype(F32) + lo_arrived[...].astype(F32)).astype(BF)
    mine[...] = jnp.where(side == 1, grad_hi, grad_lo)
    theirs[...] = jnp.where(side == 1, grad_lo, grad_hi)


def tied(value, *others):
    return lax.optimization_barrier((value, *others))[0]


def per_device(acts, grad_out, gain, gate, w_query, kept, links):
    sections = lax.axis_size("section")
    fsdps = lax.axis_size("fsdp")
    seqs = lax.axis_size("seq")
    section_idx = lax.axis_index("section")
    side = section_idx % 2
    tile, dim = acts.shape[2:]
    rows = w_query.shape[1]
    half = dim // 2
    swap_pairs = [(i, i ^ 1) for i in range(sections)]
    bits = [1 << b for b in reversed(range(seqs.bit_length() - 1))]
    top = bits[0]
    steps = [1 << b for b in reversed(range(fsdps.bit_length() - 1))]
    flips = [0]
    for step in steps:
        flips = flips + [f ^ step for f in flips]
    owners = [0]
    for step in steps:
        owners = owners + [f ^ step for f in owners]
    offsets = list(range(seqs))
    right_pairs = [(t, t + 1) for t in range(seqs - 1)]
    left_pairs = [(t + 1, t) for t in range(seqs - 1)]
    diagonal_pairs = [
        (s * seqs + t + 1, (s ^ 1) * seqs + t) for s in range(sections) for t in range(seqs - 1)
    ]
    matmul_flops = 2 * tile * dim * half
    head_flops = 2 * tile * 2 * tile * half

    def swap(value):
        return lax.ppermute(value, "section", swap_pairs)

    def across(value, offset):
        return lax.ppermute(value, "seq", [(s, s ^ offset) for s in range(seqs)])

    def along(value, flip):
        return lax.ppermute(value, "fsdp", [(f, f ^ flip) for f in range(fsdps)])

    def join(values):
        return values[0] if len(values) == 1 else jnp.concatenate(values, axis=0)

    acts_own = acts[0, 0]
    first, second = w_query[0][:, :half], w_query[0][:, half:]
    w_own, w_theirs = jnp.where(side == 0, first, second), jnp.where(side == 0, second, first)
    w_other = swap(w_theirs)
    (packed,) = call(
        pack_kernel, [sds((tile + 16, dim), BF)], 10 * tile * dim, "pack", acts_own, gain, gate
    )
    packed_in = swap(packed)

    unit = fsdps * rows
    part_shapes = [sds((seqs // 2 * unit, tile), BF)] * 2
    turned = pltpu.VMEM((dim, tile), BF)

    def to_row_owners(low, high):
        parts = [(low, [0]), (across(high, top), [0])]
        for bit in bits[1:]:
            sent = [v[b + bit * unit : b + 2 * bit * unit] for v, begins in parts for b in begins]
            arrived = across(join(sent), bit)
            parts = parts + [(arrived, [i * bit * unit for i in range(len(sent))])]
        return join([v[b : b + unit] for v, begins in parts for b in begins])

    normed_own, low_own, high_own = call(
        lambda *refs: normalize_own_kernel(offsets, rows, *refs),
        [sds((tile, dim), BF)] + part_shapes, 20 * tile * dim,
        "normalize_own", acts_own, gain, scratch=[turned],
    )
    w_hi, w_lo = call(
        select_kernel, [sds((rows, half), BF)] * 2, rows * half,
        "select_w", w_own, tied(w_other, packed, high_own),
    )
    parts_own = to_row_owners(low_own, high_own)
    def over_fsdp(shard):
        near = [shard]
        for step in steps:
            near = near + [along(join(near), step)]
        return near

    def over_seq(near, after=(), after_last=()):
        sent = [join(near[:2])] + near[2:]
        if after:
            sent = [tied(value, *after) for value in sent]
        if after_last:
            sent[-1] = tied(sent[-1], *after_last)
        return [across(value, top) for value in sent]

    def between_cores(near, far, after=(), apart=False):
        if after:
            far = [tied(value, *after) for value in far]
        places = [[(f, 0) for f in flips], [(f, top) for f in flips]]
        held = [join(near), join(far)]
        if not apart:
            held, places = [join(held)], [places[0] + places[1]]
        for bit in bits[1:]:
            held = held + [across(v, bit) for v in held]
            places = places + [[(f, o ^ bit) for f, o in place] for place in places]
        return held, places

    near_hi = over_fsdp(w_hi)
    far_hi = over_seq(near_hi, after_last=[packed_in, parts_own])
    x_hi, x_lo, normed_hi, normed_lo, keys, vecs, incoming = call(
        normalize_kernel,
        [sds((tile, dim), BF)] * 4 + [sds((2 * tile, half), BF), sds((8, dim), F32), sds((tile, half), BF)],
        30 * tile * dim,
        "normalize", acts_own, packed_in, gain, gate, grad_out[0], tied(normed_own, far_hi[0]),
    )
    left = lax.ppermute(keys, "seq", right_pairs)
    near_lo = over_fsdp(tied(w_lo, near_hi[1], packed_in))
    parts_other = swap(tied(parts_own, packed_in))
    blocks_hi, places = between_cores(near_hi, far_hi, after=[near_lo[-1], left, parts_other])
    far_lo = over_seq(near_lo, after=[left])

    def forward(name, which, normed, blocks, places):
        return call(
            lambda *refs: forward_kernel(which, places, rows, *refs),
            [sds((tile, half), BF), sds((half // HDIM * tile, 2 * tile), F32), sds((dim, half), BF)],
            matmul_flops + head_flops,
            name, normed, left, keys, *blocks, scalars=[links],
        )

    query_hi, probs_hi, weights_hi = forward("forward_hi", 0, normed_hi, blocks_hi, places)
    def over_tiles(query_grad, after=()):
        gathered = [query_grad]
        for bit in bits:
            arrived = across(join(gathered), bit)
            if after and bit == top:
                arrived = tied(arrived, *after)
            gathered = gathered + [arrived]
        return gathered

    def weight_grad(name, section_hi, gathered):
        halves = [sds((fsdps // 2 * rows, half), BF)] * 2
        return call(
            lambda *refs: weight_grad_kernel(section_hi, owners, rows, *refs),
            halves,
            2 * fsdps * rows * seqs * tile * half,
            name, parts_own, parts_other, *gathered,
            scratch=[pltpu.VMEM((fsdps * rows, half), BF)],
        )

    def over_clips(name, mine, arrived, after=()):
        if after:
            arrived = tied(arrived, *after)
        for step in reversed(steps[:-1]):
            count = mine.shape[0] // 2
            mine, sent = call(
                add_halves_kernel, [sds((count, half), BF)] * 2, 4 * count * half, name, mine, arrived
            )
            arrived = along(sent, step)
        return mine, arrived

    kept_state = None
    single = sections == 2
    for tick in range(sections // 2):
        qg_hi, own, msg, leftward, leftsum = call(
            upper_kernel,
            [
                sds((tile, half), BF),
                sds((tile, half), F32),
                sds((tile, half + HDIM), BF),
                sds((tile, half), BF),
                sds((tile, HDIM), F32),
            ],
            matmul_flops + 4 * head_flops,
            "upper", incoming, x_hi, vecs, query_hi, probs_hi, weights_hi, left, keys, scalars=[kept],
        )
        msg_in = swap(msg)
        left_in = lax.ppermute(leftward, "seq", left_pairs)
        sum_other = lax.ppermute(leftsum, ("section", "seq"), diagonal_pairs)
        exchanged = [msg_in, left_in, sum_other]
        if tick == 0:
            blocks_lo, places_lo = between_cores(near_lo, far_lo, after=exchanged, apart=True)
            query_lo, probs_lo, weights_lo = forward("forward_lo", 1, normed_lo, blocks_lo, places_lo)
        dy_mid, qg_lo, key_own, leftward_lo = call(
            lower_kernel,
            [sds((tile, half), BF), sds((tile, half), BF), sds((tile, half), F32), sds((tile, half), BF)],
            4 * head_flops,
            "lower", own, msg, msg_in, left_in, sum_other, x_hi, vecs, incoming,
            query_lo, probs_lo, left, keys, scalars=[kept],
        )
        left_in_lo = lax.ppermute(leftward_lo, "seq", left_pairs)
        dy_in = swap(dy_mid)
        if single:
            gathered_hi = over_tiles(tied(qg_hi, *exchanged), after=[qg_lo])
            mine_hi, sent_hi = weight_grad("weight_grad_hi", True, gathered_hi)
            first_hi = along(sent_hi, steps[-1])
            clips_hi = over_clips("add_pair_hi", mine_hi, first_hi)
            left_in_lo = tied(left_in_lo, clips_hi[0], dy_in)
        part_lo, msg_lo = call(
            project_kernel, [sds((tile, dim), F32), sds((tile, dim), BF)], matmul_flops,
            "project_lo", qg_lo, weights_lo, key_own, left_in_lo,
        )
        if single:
            gathered_lo = over_tiles(qg_lo, after=[first_hi])
            gathered_lo[-1] = tied(gathered_lo[-1], clips_hi[0])
            mine_lo, sent_lo = weight_grad("weight_grad_lo", False, gathered_lo)
            first_lo = along(sent_lo, steps[-1])
            clips_lo = over_clips("add_pair_lo", mine_lo, first_lo, after=clips_hi[1:])
        msg_lo_in = lax.ppermute(msg_lo, "section", [(i + 1, i) for i in range(0, sections, 2)])
        (updated,) = call(
            finish_kernel, [sds((tile, dim), BF)], 20 * tile * dim,
            "finish", part_lo, msg_lo_in, x_lo, vecs, dy_mid, dy_in, scalars=[kept],
        )
        state = (updated, qg_hi, qg_lo)
        if kept_state is None:
            kept_state = state
        else:
            active = section_idx // 2 == sections // 2 - 1 - tick
            kept_state = jax.tree.map(lambda new, old: jnp.where(active, new, old), state, kept_state)
        if tick + 1 < sections // 2:
            to_low = lax.ppermute(updated[:, :half], "section", [(i, i - 2) for i in range(2, sections, 2)])
            to_high = lax.ppermute(updated[:, half:], "section", [(i, i - 1) for i in range(2, sections, 2)])
            incoming = jnp.where(side == 0, to_low, to_high)
    result, qg_hi, qg_lo = kept_state
    if not single:
        clips = []
        for name, section_hi, query_grad in (("hi", True, qg_hi), ("lo", False, qg_lo)):
            mine, sent = weight_grad("weight_grad_" + name, section_hi, over_tiles(query_grad))
            clips.append(over_clips("add_pair_" + name, mine, along(sent, steps[-1])))
        clips_hi, clips_lo = clips

    mine, theirs = call(
        add_kernel, [sds((rows, half), BF)] * 2, 20 * rows * half,
        "add_clips", *clips_hi, *clips_lo,
    )
    other = swap(theirs)
    first = jnp.where(side == 0, mine, other)
    second = jnp.where(side == 0, other, mine)
    grad_rows = jnp.concatenate([first, second], axis=1)
    return (result[None, None], grad_rows[None])


def solution(mesh):
    placed = (
        P("section", "fsdp", "seq", None),
        P("fsdp", "seq", None),
        P("section", None),
        P("section", None),
        P("section", ("fsdp", "seq"), None),
        P("fsdp", None),
        P("fsdp", "seq"),
    )
    return jax.shard_map(
        per_device,
        mesh=mesh,
        in_specs=placed,
        out_specs=(P("section", "fsdp", "seq", None), P("section", ("fsdp", "seq"), None)),
        check_vma=False,
    )
```
